256 devices in a mesh: blk: 32 (over z, x_hi, core), tensor: 8 (over y, x_lo).
Axes of the slice: x: 4 (x_hi: 2, x_lo: 2; x = x_hi * 2 + x_lo), y: 4, z: 8, core: 2. Of those that a mesh axis runs over, the one named last changes fastest.
Arguments:
- queries: bfloat16 [16384, 2048], P('blk', 'tensor'), may hold values from -5 to 5
- key_states: bfloat16 [16384, 2048], P('blk', 'tensor'), may hold values from -5 to 5
- value_states: bfloat16 [16384, 2048], P('blk', 'tensor'), may hold values from -6 to 6
- out_weight: bfloat16 [2048, 4096], P('tensor'), may hold values from -0.1875 to 0.1875
- lengths: int32 [32], replicated, may hold values from 128 to 512, as said below
- cycle_order: int32 [32], replicated, may hold values from 0 to 31, each once
Outputs:
- mixed_out: bfloat16 [16384, 4096], P('blk', 'tensor')
The draws below stay inside these ranges and needn't reach their ends.
Inputs may be any that keep to these rules, and one draw needn't show every extreme that they name: lengths are multiples of 128; some slice is full and some holds exactly 128 tokens. `cycle_order`: each slice number appears once.
All inputs are finite; a program needn't handle non-finite values.
Results may differ from the reference program's by a relative error of at most 0.009.
Values may be sent and summed in bfloat16 or wider, within the bound.
A program may use at most 128 MiB of HBM per device.

```python
import jax
import jax.numpy as jnp
from jax import lax

D = 4096
HD = 128
HEADS = 16
UNIT = 128
CAP = 512
CYCLE = 32
TOKENS = 16384
N_BLK = 32
N_TENSOR = 8


def draw_queries(key, part):
    key = jax.random.fold_in(key, 3)
    sampled = jnp.clip(1.5 * jax.random.normal(key, (TOKENS, HEADS * HD), jnp.float32), -5.0, 5.0)
    return sampled.astype(jnp.bfloat16)


def draw_key_states(key, part):
    key = jax.random.fold_in(key, 4)
    sampled = jnp.clip(1.5 * jax.random.normal(key, (TOKENS, HEADS * HD), jnp.float32), -5.0, 5.0)
    return sampled.astype(jnp.bfloat16)


def draw_lengths(key, part):
    key = jax.random.fold_in(key, 5)
    unit_counts = jax.random.randint(jax.random.fold_in(key, 1), (CYCLE,), 1, CAP // UNIT + 1)
    full_pick = jax.random.randint(jax.random.fold_in(key, 2), (), 0, CYCLE)
    short_pick = (full_pick + jax.random.randint(jax.random.fold_in(key, 3), (), 1, CYCLE)) % CYCLE
    unit_counts = unit_counts.at[full_pick].set(CAP // UNIT)
    unit_counts = unit_counts.at[short_pick].set(1)
    return (unit_counts * UNIT).astype(jnp.int32)


def with_spikes(values, rng, source, target, shards_of, factor):
    owner, partner = [(jnp.arange(values.shape[dim]) // (values.shape[dim] // shards_of)).reshape([-1 if axis == dim else 1 for axis in range(values.ndim)]) for dim in (source, target)]
    chosen = jax.random.permutation(rng, shards_of)[partner]
    strong = (owner == chosen) | (owner == (partner + shards_of // 2) % shards_of)
    return jnp.where(strong, factor * values, values)


def block_scale(own_key, shape, split, smallest, largest):
    gain = 1.0
    for axis_at, parts in split:
        draws = jax.random.uniform(jax.random.fold_in(jax.random.fold_in(own_key, 6), axis_at), (parts,), jnp.float32, smallest / len(split), largest / len(split))
        gain = gain * jnp.repeat(jnp.exp(draws), shape[axis_at] // parts).reshape((-1,) + (1,) * (len(shape) - 1 - axis_at))
    return gain


def gaussian(key, shape, deviation, limit, split=(), held_as=jnp.bfloat16):
    result = jax.random.normal(key, shape, jnp.float32) * deviation
    if len(split) > 0:
        result = block_scale(key, shape, split, -0.22, 0.18) * result
    return jnp.clip(result, min=-limit, max=limit).astype(held_as)


def noise_with(own_key, shape, deviation, reach, cuts, heavy, kind=jnp.bfloat16):
    entries = deviation * jax.random.normal(own_key, shape, jnp.float32)
    if cuts:
        entries = entries * block_scale(own_key, shape, cuts, -0.22, 0.18)
    return jnp.clip(with_spikes(entries, jax.random.fold_in(own_key, 3), *heavy), -reach, reach).astype(kind)


def setup_inputs(seed: int = 0) -> dict:
    seeds = jax.random.split(jax.random.key(seed), 7)
    queries = draw_queries(jax.random.fold_in(seeds[6], 71), 0)
    key_states = draw_key_states(jax.random.fold_in(seeds[6], 71), 0)
    value_states = gaussian(seeds[2], (TOKENS, HEADS * HD), 1.0, 6.0, ((0, 32), (1, 8)))
    out_weight = noise_with(seeds[3], (HEADS * HD, D), (HEADS * HD) ** -0.5, 0.1875, ((0, 8),), (0, 1, 8, 2.0))
    lengths = draw_lengths(jax.random.fold_in(seeds[6], 71), 0)
    cycle_order = jax.random.permutation(seeds[5], CYCLE).astype(jnp.int32)
    return {"queries": queries, "key_states": key_states, "value_states": value_states, "out_weight": out_weight, "lengths": lengths, "cycle_order": cycle_order}


NEG_FILL = -1.0e30


def slice_starts(lengths, cycle_order):
    before = (cycle_order[None, :] < cycle_order[:, None]).astype(jnp.int32)
    return jnp.sum(before * lengths[None, :], axis=1).astype(jnp.int32)


def reference(queries, key_states, value_states, out_weight, lengths, cycle_order):
    starts = slice_starts(lengths, cycle_order)
    row_index = jnp.arange(TOKENS, dtype=jnp.int32)
    holder = row_index // CAP
    offset = row_index % CAP
    positions = starts[holder] + offset
    is_valid = offset < lengths[holder]
    query_heads = queries.reshape(TOKENS, HEADS, HD)
    key_heads = key_states.reshape(TOKENS, HEADS, HD)
    value_heads = value_states.reshape(TOKENS, HEADS, HD)
    score_scale = HD ** -0.5

    def head_block(work_item):
        block_pick = work_item // HEADS
        head_pick = work_item % HEADS
        first_row = (block_pick * CAP).astype(jnp.int32)
        zero_index = jnp.zeros((), jnp.int32)
        query_rows = lax.dynamic_slice(query_heads, (first_row, head_pick, zero_index), (CAP, 1, HD))[:, 0, :]
        key_rows = lax.dynamic_index_in_dim(key_heads, head_pick, 1, keepdims=False)
        value_rows = lax.dynamic_index_in_dim(value_heads, head_pick, 1, keepdims=False)
        query_pos = lax.dynamic_slice_in_dim(positions, first_row, CAP)
        query_valid = lax.dynamic_slice_in_dim(is_valid, first_row, CAP)
        scores = jnp.dot(query_rows, key_rows.T, preferred_element_type=jnp.float32) * score_scale
        allowed = query_valid[:, None] & is_valid[None, :] & (positions[None, :] <= query_pos[:, None])
        masked = jnp.where(allowed, scores, NEG_FILL)
        row_max = jnp.max(masked, axis=1, keepdims=True)
        weights = jnp.where(allowed, jnp.exp(masked - row_max), 0.0)
        row_sum = jnp.sum(weights, axis=1)
        summed = jnp.dot(weights.astype(jnp.bfloat16), value_rows, preferred_element_type=jnp.float32)
        safe_sum = jnp.where(query_valid, row_sum, 1.0)
        return jnp.where(query_valid[:, None], summed / safe_sum[:, None], 0.0).astype(jnp.bfloat16)

    attended = lax.map(head_block, jnp.arange(N_BLK * HEADS, dtype=jnp.int32))
    attended = attended.reshape(N_BLK, HEADS, CAP, HD).transpose(0, 2, 1, 3).reshape(TOKENS, HEADS * HD)
    group_width = HEADS * HD // N_TENSOR
    accumulated = jnp.zeros((TOKENS, D), jnp.float32)
    for group_index in range(N_TENSOR):
        low_col = group_index * group_width
        partial_value = jnp.dot(attended[:, low_col:low_col + group_width], out_weight[low_col:low_col + group_width], preferred_element_type=jnp.float32)
        accumulated = accumulated + partial_value
    return accumulated.astype(jnp.bfloat16)
```

```python
import math

import jax
import jax.numpy as jnp
from jax import lax
from jax.experimental import pallas as pl
from jax.experimental.pallas import tpu as pltpu
from jax.sharding import PartitionSpec as P

HD = 128
UNIT = 128
CAP = 512
N_Z = 8
N_TENSOR = 8
N_BLK = 32
ROWS = 2 * CAP
TILE = 256
NEG = -(2.0**100)
EXP_SCALE = math.log2(math.e) / math.sqrt(HD)
MESH = pl.DeviceIdType.MESH
NT = (((1,), (1,)), ((), ()))


def block_of(z, h, c):
    return lax.rem(z, N_Z) * 4 + h * 2 + c


def kernel(
    q_ref, k_ref, v_ref, w_ref, len_ref, ord_ref, out_ref,
    kv, q2, acc, top, bias, ob, og, wb, total,
    loc, par_s, par_r, ring_s, ring_r, sib_s, sib_r, w_s, w_r, o_s, o_r,
):
    b = lax.axis_index("blk")
    t = lax.axis_index("tensor")
    z = b // 4
    h = lax.rem(b // 2, 2)
    c = lax.rem(b, 2)
    other_b = block_of(z, 1 - h, c)
    sibling = {"blk": block_of(z, h, 1 - c), "tensor": t}
    partner = {"blk": other_b, "tensor": t}
    z_up = {"blk": block_of(z + 1, h, c), "tensor": t}
    z_down = {"blk": block_of(z + N_Z - 1, h, c), "tensor": t}
    my_cols = pl.ds(pl.multiple_of(h * HD, HD), HD)
    other_cols = pl.ds(pl.multiple_of((1 - h) * HD, HD), HD)
    my_head = 2 * t + h

    def tensor_at(step):
        return lax.rem(t + step, N_TENSOR)

    def remote(src, dst, send, recv, device):
        return pltpu.make_async_remote_copy(
            src_ref=src, dst_ref=dst, send_sem=send, recv_sem=recv,
            device_id=device, device_id_type=MESH,
        )

    own = [
        pltpu.make_async_copy(k_ref.at[:, my_cols], kv.at[b, 0], loc.at[0]),
        pltpu.make_async_copy(v_ref.at[:, my_cols], kv.at[b, 1], loc.at[1]),
        pltpu.make_async_copy(q_ref.at[:, my_cols], q2.at[pl.ds(0, CAP), pl.ds(0, HD)], loc.at[2]),
        pltpu.make_async_copy(
            w_ref.at[
                pl.ds(pl.multiple_of(c * HD, HD), HD), pl.ds(pl.multiple_of(t * CAP, CAP), CAP)
            ],
            wb.at[2 * t + c],
            loc.at[3],
        ),
    ]
    for copy in own:
        copy.start()

    barrier = pltpu.get_barrier_semaphore()
    peers = [z_up, z_down, sibling]
    peers += [{"blk": b, "tensor": tensor_at(d)} for d in range(1, N_TENSOR)]
    peers += [{"blk": other_b, "tensor": tensor_at(d)} for d in range(N_TENSOR)]
    for peer in peers:
        pl.semaphore_signal(barrier, inc=1, device_id=peer, device_id_type=MESH)

    lane = lax.broadcasted_iota(jnp.int32, (UNIT, 128), 1)
    row = lax.broadcasted_iota(jnp.int32, (UNIT, 128), 0)
    lengths = jnp.broadcast_to(len_ref[...].astype(jnp.float32), (UNIT, 128))
    orders = jnp.broadcast_to(ord_ref[...].astype(jnp.float32), (UNIT, 128))
    holder = lane == row // 4
    unit_start = (lax.rem(row, 4) * UNIT).astype(jnp.float32)
    my_len = jnp.sum(jnp.where(holder, lengths, 0.0), axis=1, keepdims=True)
    my_order = jnp.sum(jnp.where(holder, orders, 0.0), axis=1, keepdims=True)
    before = jnp.where((orders < my_order) & (lane < N_BLK), lengths, 0.0)
    position = jnp.sum(before, axis=1, keepdims=True) + unit_start
    is_live = unit_start < my_len
    query_unit = jnp.where(lane < 4, b * 4 + lane, other_b * 4 + lane - 4)
    chosen = (query_unit == row) & (lane < 8)
    query_position = jnp.sum(jnp.where(chosen, position, 0.0), axis=0, keepdims=True)
    query_live = jnp.sum(jnp.where(chosen & is_live, 1.0, 0.0), axis=0, keepdims=True)
    bias[...] = jnp.where(is_live & (position < query_position), 0.0, NEG)
    tile_row = lax.broadcasted_iota(jnp.int32, (ROWS, HD), 0) // UNIT
    tile_lane = lax.broadcasted_iota(jnp.int32, (ROWS, HD), 1)
    q2[:, HD:] = jnp.where(tile_row == tile_lane, 1.0, 0.0).astype(jnp.bfloat16)

    pl.semaphore_wait(barrier, len(peers))
    for copy in own:
        copy.wait()

    def ring_copy(slot, part, way, step):
        index = part * 8 + way * 4 + step
        device = z_up if way == 0 else z_down
        return remote(kv.at[slot], kv.at[slot], ring_s.at[index], ring_r.at[index], device)

    def sib_copy(slot, index):
        return remote(kv.at[slot], kv.at[slot], sib_s.at[index], sib_r.at[index], sibling)

    ring_copy(b, 0, 0, 0).start()
    ring_copy(b, 0, 1, 0).start()
    swaps = [
        remote(k_ref.at[:, other_cols], kv.at[b, 0], par_s.at[0], par_r.at[0], partner),
        remote(v_ref.at[:, other_cols], kv.at[b, 1], par_s.at[1], par_r.at[1], partner),
        remote(
            q_ref.at[:, other_cols],
            q2.at[pl.ds(CAP, CAP), pl.ds(0, HD)],
            par_s.at[2],
            par_r.at[2],
            partner,
        ),
    ]
    for copy in swaps:
        copy.start()
    sib_copy(b, 0).start()

    square_row = lax.broadcasted_iota(jnp.int32, (UNIT, UNIT), 0)
    square_lane = lax.broadcasted_iota(jnp.int32, (UNIT, UNIT), 1)

    def diagonal(slot, first):
        def unit(i, carry):
            rows = pl.ds(pl.multiple_of((first + i) * UNIT, UNIT), UNIT)
            keys = pl.ds(pl.multiple_of(i * UNIT, UNIT), UNIT)
            k = kv[slot, 0, keys, :]
            v = kv[slot, 1, keys, :]
            s = lax.dot_general(q2[rows, :HD], k, NT, preferred_element_type=jnp.float32)
            s = jnp.where(square_lane <= square_row, s, NEG)
            best = jnp.broadcast_to(jnp.max(s, axis=1, keepdims=True), (UNIT, HD))
            p = jnp.exp2((s - best) * EXP_SCALE).astype(jnp.bfloat16)
            top[rows, :] = best
            acc[rows, :] = jnp.dot(
                p,
                jnp.concatenate([v, jnp.ones_like(v)], axis=1),
                preferred_element_type=jnp.float32,
            )
            return carry

        lax.fori_loop(0, 4, unit, 0)

    diagonal(b, 0)
    remote(kv.at[b, 0], kv.at[other_b, 0], par_s.at[0], par_r.at[0], partner).wait_recv()
    remote(kv.at[b, 1], kv.at[other_b, 1], par_s.at[1], par_r.at[1], partner).wait_recv()
    ring_copy(other_b, 1, 0, 0).start()
    ring_copy(other_b, 1, 1, 0).start()
    sib_copy(other_b, 8).start()
    swaps[2].wait_recv()
    diagonal(other_b, 4)

    def w_copy(step):
        target = tensor_at(step)
        return remote(
            w_ref.at[
                pl.ds(pl.multiple_of(c * HD, HD), HD), pl.ds(pl.multiple_of(target * CAP, CAP), CAP)
            ],
            wb.at[2 * t + c],
            w_s.at[step - 1],
            w_r.at[step - 1],
            {"blk": b, "tensor": target},
        )

    def w_arrived(step):
        source = tensor_at(N_TENSOR - step)
        slot = wb.at[2 * source + c]
        remote(slot, slot, w_s.at[step - 1], w_r.at[step - 1], sibling).wait_recv()

    def w_sib(j):
        slot = wb.at[2 * j + c]
        return remote(slot, slot, w_s.at[7 + j], w_r.at[7 + j], sibling)

    def w_sib_arrived(j):
        slot = wb.at[2 * j + 1 - c]
        remote(slot, slot, w_s.at[7 + j], w_r.at[7 + j], sibling).wait_recv()

    def attend(slot_x, slot_y):
        keys = jnp.concatenate([kv[slot_x, 0], kv[slot_y, 0]], axis=0)
        values = jnp.concatenate([kv[slot_x, 1], kv[slot_y, 1]], axis=0)
        fills = []
        for slot in (slot_x, slot_y):
            for j in range(4):
                fills.append(jnp.broadcast_to(bias[pl.ds(slot * 4 + j, 1), :], (UNIT, HD)))
        keys = jnp.concatenate([keys, jnp.concatenate(fills, axis=0).astype(jnp.bfloat16)], axis=1)
        values = jnp.concatenate([values, jnp.ones_like(values)], axis=1)
        for i in range(ROWS // TILE):
            rows = pl.ds(i * TILE, TILE)
            s = lax.dot_general(q2[rows, :], keys, NT, preferred_element_type=jnp.float32)
            old = top[rows, :]
            best = jnp.maximum(old, jnp.max(s, axis=1, keepdims=True))
            shrink = jnp.exp2((old - best) * EXP_SCALE)
            top[rows, :] = best
            p = jnp.concatenate(
                [
                    jnp.exp2((s[:, j * 128 : (j + 1) * 128] - best) * EXP_SCALE).astype(
                        jnp.bfloat16
                    )
                    for j in range(s.shape[1] // 128)
                ],
                axis=1,
            )
            update = jnp.dot(p, values, preferred_element_type=jnp.float32)
            acc[rows, :] = acc[rows, :] * jnp.concatenate([shrink, shrink], axis=1) + update

    def ring_step(s, part, way):
        side = lax.rem(h + part, 2)
        slot = block_of(z + (N_Z - s if way == 0 else s), side, c)
        ring_copy(slot, part, way, s - 1).wait_recv()
        reach = 4 if part == way else 3

        @pl.when(s < reach)
        def _():
            ring_copy(slot, part, way, s).start()

        sib_copy(slot, part * 8 + (N_Z - s if way == 0 else s)).start()

    def sib_wait(part, distance):
        side = lax.rem(h + part, 2)
        slot = block_of(z + distance, side, 1 - c)
        sib_copy(slot, part * 8 + distance).wait_recv()

    def distance_step(s, carry):
        single = 1 - (lax.rem(s, 4) + 3) // 4

        def phase(ph, inner):
            part = ph // 2
            core = lax.rem(c + ph, 2)

            @pl.when((s > 0) & (s < 4) & (lax.rem(ph, 2) == 0))
            def _():
                ring_step_both(s, part)

            @pl.when((s > 0) & (s < 4) & (lax.rem(ph, 2) == 1))
            def _():
                sib_wait(part, N_Z - s)
                sib_wait(part, s)

            @pl.when((s == 4) & (ph == 0))
            def _():
                ring_step(s, 0, 0)
                ring_step(s, 1, 1)

            @pl.when(((s == 4) | (s == 0)) & (ph == 1))
            def _():
                sib_wait(0, s)
                sib_wait(1, s)

            @pl.when((s == 1) & (ph == 0))
            def _():
                for step in range(1, N_TENSOR):
                    w_copy(step).start()

            @pl.when((s == 3) & (ph == 3))
            def _():
                for step in range(1, N_TENSOR):
                    w_arrived(step)
                for j in range(N_TENSOR):
                    w_sib(j).start()

            side_x = lax.rem(h + part, 2)
            side_y = lax.rem(h + part + single, 2)
            attend(block_of(z + N_Z - s, side_x, core), block_of(z + s, side_y, core))
            return inner

        lax.fori_loop(0, 4 - 2 * single, phase, 0)
        return carry

    def ring_step_both(s, part):
        for p in range(2):

            @pl.when(part == p)
            def _():
                ring_step(s, p, 0)
                ring_step(s, p, 1)

    lax.fori_loop(0, 5, distance_step, 0)

    def finish(half):
        for i in range(4):
            rows = pl.ds(half * CAP + i * UNIT, UNIT)
            unit_live = jnp.sum(
                jnp.where(lane[:1, :] == half * 4 + i, query_live, 0.0), axis=1, keepdims=True
            )
            o = jnp.where(unit_live > 0.0, acc[rows, :HD] / acc[rows, HD:], 0.0)
            ob[half, pl.ds(i * UNIT, UNIT), :] = o.astype(jnp.bfloat16)

    def o_copy(half, step):
        index = half * 7 + step if half else step - 1
        device = {"blk": other_b if half else b, "tensor": tensor_at(step)}
        return remote(ob.at[half], og.at[my_head], o_s.at[index], o_r.at[my_head], device)

    finish(1)
    for step in range(N_TENSOR):
        o_copy(1, step).start()
    finish(0)
    for step in range(1, N_TENSOR):
        o_copy(0, step).start()
    og[my_head] = ob[0]
    for j in range(N_TENSOR):
        w_sib_arrived(j)

    def arrived(head):
        remote(ob.at[0], og.at[head], o_s.at[0], o_r.at[head], partner).wait_recv()

    total[...] = jnp.zeros_like(total)
    for step in range(N_TENSOR):
        j = tensor_at(step)
        if step > 0:
            arrived(2 * j + h)
        arrived(2 * j + 1 - h)
        rows = jnp.concatenate([og[2 * j], og[2 * j + 1]], axis=1)
        weight = jnp.concatenate([wb[2 * j], wb[2 * j + 1]], axis=0)
        total[...] += jnp.dot(rows, weight, preferred_element_type=jnp.float32)
    out_ref[...] = total[...].astype(jnp.bfloat16)

    for copy in swaps:
        copy.wait_send()
    for step in range(1, N_TENSOR):
        w_copy(step).wait_send()
        o_copy(0, step).wait_send()
    for step in range(N_TENSOR):
        w_sib(step).wait_send()
        o_copy(1, step).wait_send()

    def sent(index, carry):
        sib_copy(0, index).wait_send()
        return carry

    lax.fori_loop(0, 16, sent, 0)
    for part in range(2):
        for way in range(2):
            for step in range(4 if part == way else 3):
                ring_copy(0, part, way, step).wait_send()


def body(queries, key_states, value_states, out_weight, lengths, cycle_order):
    pad = lambda a: jnp.pad(a, (0, 128 - N_BLK)).reshape(1, 128)
    any_space = pl.BlockSpec(memory_space=pl.ANY)
    vmem = pl.BlockSpec(memory_space=pltpu.VMEM)
    dma = pltpu.SemaphoreType.DMA
    return pl.pallas_call(
        kernel,
        out_shape=jax.ShapeDtypeStruct((CAP, CAP), jnp.bfloat16),
        in_specs=[any_space] * 4 + [vmem] * 2,
        out_specs=vmem,
        scratch_shapes=[
            pltpu.VMEM((N_BLK, 2, CAP, HD), jnp.bfloat16),
            pltpu.VMEM((ROWS, 2 * HD), jnp.bfloat16),
            pltpu.VMEM((ROWS, 2 * HD), jnp.float32),
            pltpu.VMEM((ROWS, HD), jnp.float32),
            pltpu.VMEM((UNIT, 128), jnp.float32),
            pltpu.VMEM((2, CAP, HD), jnp.bfloat16),
            pltpu.VMEM((2 * N_TENSOR, CAP, HD), jnp.bfloat16),
            pltpu.VMEM((2 * N_TENSOR, HD, CAP), jnp.bfloat16),
            pltpu.VMEM((CAP, CAP), jnp.float32),
            dma((4,)),
            dma((3,)),
            dma((3,)),
            dma((16,)),
            dma((16,)),
            dma((16,)),
            dma((16,)),
            dma((15,)),
            dma((15,)),
            dma((15,)),
            dma((16,)),
        ],
        compiler_params=pltpu.CompilerParams(
            collective_id=0, has_side_effects=True, vmem_limit_bytes=56 * 2**20
        ),
        name="ring_attention",
    )(queries, key_states, value_states, out_weight, pad(lengths), pad(cycle_order))


def solution(mesh):
    placed = (
        P("blk", "tensor"),
        P("blk", "tensor"),
        P("blk", "tensor"),
        P("tensor", None),
        P(),
        P(),
    )
    return jax.shard_map(
        body, mesh=mesh, in_specs=placed, out_specs=P("blk", "tensor"), check_vma=False
    )
```

```python
import functools
import math

import jax
import jax.numpy as jnp
from jax import lax
from jax.experimental import pallas as pl
from jax.experimental.pallas import tpu as pltpu
from jax.sharding import PartitionSpec as P

HD = 128
UNIT = 128
CAP = 512
N_Z = 8
N_TENSOR = 8
N_BLK = 32
ROWS = 2 * CAP
TILE = 256
NEG = -(2.0**100)
EXP_SCALE = math.log2(math.e) / math.sqrt(HD)
MESH = pl.DeviceIdType.MESH
NT = (((1,), (1,)), ((), ()))


def block_of(z, h, c):
    return lax.rem(z, N_Z) * 4 + h * 2 + c


def kernel(
    q_ref, k_ref, v_ref, w_ref, len_ref, ord_ref, out_ref,
    kv, q2, acc, top, bias, ob, og, wb, total, transit,
    loc, par_s, par_r, ring_s, ring_r, sib_s, sib_r, w_s, w_r, o_s, o_r, t_r,
):
    b = lax.axis_index("blk")
    t = lax.axis_index("tensor")
    z = b // 4
    h = lax.rem(b // 2, 2)
    c = lax.rem(b, 2)
    y = t // 2
    x_lo = lax.rem(t, 2)
    other_b = block_of(z, 1 - h, c)
    sibling = {"blk": block_of(z, h, 1 - c), "tensor": t}
    partner = {"blk": other_b, "tensor": t}
    z_up = {"blk": block_of(z + 1, h, c), "tensor": t}
    z_down = {"blk": block_of(z + N_Z - 1, h, c), "tensor": t}
    my_cols = pl.ds(pl.multiple_of(h * HD, HD), HD)
    other_cols = pl.ds(pl.multiple_of((1 - h) * HD, HD), HD)
    my_head = 2 * t + h

    def tensor_at(step):
        return lax.rem(t + step, N_TENSOR)

    def remote(src, dst, send, recv, device):
        return pltpu.make_async_remote_copy(
            src_ref=src, dst_ref=dst, send_sem=send, recv_sem=recv,
            device_id=device, device_id_type=MESH,
        )

    own = [
        pltpu.make_async_copy(k_ref.at[:, my_cols], kv.at[b, 0], loc.at[0]),
        pltpu.make_async_copy(v_ref.at[:, my_cols], kv.at[b, 1], loc.at[1]),
        pltpu.make_async_copy(q_ref.at[:, my_cols], q2.at[pl.ds(0, CAP), pl.ds(0, HD)], loc.at[2]),
        pltpu.make_async_copy(
            w_ref.at[
                pl.ds(pl.multiple_of(c * HD, HD), HD), pl.ds(pl.multiple_of(t * CAP, CAP), CAP)
            ],
            wb.at[2 * t + c],
            loc.at[3],
        ),
    ]
    for copy in own:
        copy.start()

    barrier = pltpu.get_barrier_semaphore()
    peers = [z_up, z_down, sibling]
    peers += [{"blk": b, "tensor": tensor_at(d)} for d in range(1, N_TENSOR)]
    peers += [{"blk": other_b, "tensor": 2 * y + side} for side in range(2)]
    for peer in peers:
        pl.semaphore_signal(barrier, inc=1, device_id=peer, device_id_type=MESH)

    lane = lax.broadcasted_iota(jnp.int32, (UNIT, 128), 1)
    row = lax.broadcasted_iota(jnp.int32, (UNIT, 128), 0)
    lengths = jnp.broadcast_to(len_ref[...].astype(jnp.float32), (UNIT, N_BLK))
    orders = jnp.broadcast_to(ord_ref[...].astype(jnp.float32), (UNIT, N_BLK))
    holder = lane[:, :N_BLK] == row[:, :N_BLK] // 4
    unit_start = (lax.rem(row[:, :1], 4) * UNIT).astype(jnp.float32)
    my_len = jnp.sum(jnp.where(holder, lengths, 0.0), axis=1, keepdims=True)
    my_order = jnp.sum(jnp.where(holder, orders, 0.0), axis=1, keepdims=True)
    before = jnp.where(orders < my_order, lengths, 0.0)
    position = jnp.sum(before, axis=1, keepdims=True) + unit_start
    is_live = unit_start < my_len
    query_unit = jnp.where(lane < 4, b * 4 + lane, other_b * 4 + lane - 4)
    chosen = (query_unit == row) & (lane < 8)
    query_position = jnp.sum(jnp.where(chosen, position, 0.0), axis=0, keepdims=True)
    query_live = jnp.sum(jnp.where(chosen & is_live, 1.0, 0.0), axis=0, keepdims=True)
    bias[...] = jnp.where(is_live & (position < query_position), 0.0, NEG)
    tile_row = lax.broadcasted_iota(jnp.int32, (ROWS, HD), 0) // UNIT
    tile_lane = lax.broadcasted_iota(jnp.int32, (ROWS, HD), 1)
    q2[:, HD:] = jnp.where(tile_row == tile_lane, 1.0, 0.0).astype(jnp.bfloat16)

    pl.semaphore_wait(barrier, len(peers))
    for copy in own:
        copy.wait()

    def ring_copy(slot, part, way, step):
        index = part * 8 + way * 4 + step
        device = z_up if way == 0 else z_down
        return remote(kv.at[slot], kv.at[slot], ring_s.at[index], ring_r.at[index], device)

    def sib_copy(slot, index):
        return remote(kv.at[slot], kv.at[slot], sib_s.at[index], sib_r.at[index], sibling)

    ring_copy(b, 0, 0, 0).start()
    ring_copy(b, 0, 1, 0).start()
    swaps = [
        remote(k_ref.at[:, other_cols], kv.at[b, 0], par_s.at[0], par_r.at[0], partner),
        remote(v_ref.at[:, other_cols], kv.at[b, 1], par_s.at[1], par_r.at[1], partner),
        remote(
            q_ref.at[:, other_cols],
            q2.at[pl.ds(CAP, CAP), pl.ds(0, HD)],
            par_s.at[2],
            par_r.at[2],
            partner,
        ),
    ]
    swaps[0].start()
    swaps[1].start()
    sib_copy(b, 0).start()

    square_row = lax.broadcasted_iota(jnp.int32, (UNIT, UNIT), 0)
    square_lane = lax.broadcasted_iota(jnp.int32, (UNIT, UNIT), 1)

    def diagonal(slot, first):
        def unit(i, carry):
            rows = pl.ds(pl.multiple_of((first + i) * UNIT, UNIT), UNIT)
            keys = pl.ds(pl.multiple_of(i * UNIT, UNIT), UNIT)
            k = kv[slot, 0, keys, :]
            v = kv[slot, 1, keys, :]
            s = lax.dot_general(q2[rows, :HD], k, NT, preferred_element_type=jnp.float32)
            s = jnp.where(square_lane <= square_row, s, NEG)
            best = jnp.broadcast_to(jnp.max(s, axis=1, keepdims=True), (UNIT, HD))
            p = jnp.exp2((s - best) * EXP_SCALE).astype(jnp.bfloat16)
            top[rows, :] = best
            acc[rows, :] = jnp.dot(
                p,
                jnp.concatenate([v, jnp.ones_like(v)], axis=1),
                preferred_element_type=jnp.float32,
            )
            return carry

        lax.fori_loop(0, 4, unit, 0)

    diagonal(b, 0)
    swaps[2].start()
    remote(kv.at[b, 0], kv.at[other_b, 0], par_s.at[0], par_r.at[0], partner).wait_recv()
    remote(kv.at[b, 1], kv.at[other_b, 1], par_s.at[1], par_r.at[1], partner).wait_recv()
    ring_copy(other_b, 1, 0, 0).start()
    ring_copy(other_b, 1, 1, 0).start()
    sib_copy(other_b, 8).start()
    swaps[2].wait_recv()
    diagonal(other_b, 4)

    def w_copy(step):
        target = tensor_at(step)
        return remote(
            w_ref.at[
                pl.ds(pl.multiple_of(c * HD, HD), HD), pl.ds(pl.multiple_of(target * CAP, CAP), CAP)
            ],
            wb.at[2 * t + c],
            w_s.at[step - 1],
            w_r.at[step - 1],
            {"blk": b, "tensor": target},
        )

    def w_arrived(step):
        source = tensor_at(N_TENSOR - step)
        slot = wb.at[2 * source + c]
        remote(slot, slot, w_s.at[step - 1], w_r.at[step - 1], sibling).wait_recv()

    def w_sib(j):
        slot = wb.at[2 * j + c]
        return remote(slot, slot, w_s.at[7 + j], w_r.at[7 + j], sibling)

    def w_sib_arrived(j):
        slot = wb.at[2 * j + 1 - c]
        remote(slot, slot, w_s.at[7 + j], w_r.at[7 + j], sibling).wait_recv()

    def attend(slot_x, slot_y):
        keys = jnp.concatenate([kv[slot_x, 0], kv[slot_y, 0]], axis=0)
        values = jnp.concatenate([kv[slot_x, 1], kv[slot_y, 1]], axis=0)
        fills = []
        for slot in (slot_x, slot_y):
            for j in range(4):
                fills.append(jnp.broadcast_to(bias[pl.ds(slot * 4 + j, 1), :], (UNIT, HD)))
        keys = jnp.concatenate([keys, jnp.concatenate(fills, axis=0).astype(jnp.bfloat16)], axis=1)
        values = jnp.concatenate([values, jnp.ones_like(values)], axis=1)
        for i in range(ROWS // TILE):
            rows = pl.ds(i * TILE, TILE)
            s = lax.dot_general(q2[rows, :], keys, NT, preferred_element_type=jnp.float32)
            old = top[rows, :]
            best = jnp.maximum(old, jnp.max(s, axis=1, keepdims=True))
            shrink = jnp.exp2((old - best) * EXP_SCALE)
            top[rows, :] = best
            p = jnp.concatenate(
                [
                    jnp.exp2((s[:, j * 128 : (j + 1) * 128] - best) * EXP_SCALE).astype(
                        jnp.bfloat16
                    )
                    for j in range(s.shape[1] // 128)
                ],
                axis=1,
            )
            update = jnp.dot(p, values, preferred_element_type=jnp.float32)
            acc[rows, :] = acc[rows, :] * jnp.concatenate([shrink, shrink], axis=1) + update

    def ring_step(s, part, way):
        side = lax.rem(h + part, 2)
        slot = block_of(z + (N_Z - s if way == 0 else s), side, c)
        ring_copy(slot, part, way, s - 1).wait_recv()
        reach = 4 if part == way else 3

        @pl.when(s < reach)
        def _():
            ring_copy(slot, part, way, s).start()

        sib_copy(slot, part * 8 + (N_Z - s if way == 0 else s)).start()

    def sib_wait(part, distance):
        side = lax.rem(h + part, 2)
        slot = block_of(z + distance, side, 1 - c)
        sib_copy(slot, part * 8 + distance).wait_recv()

    def distance_step(s, carry):
        single = 1 - (lax.rem(s, 4) + 3) // 4

        def phase(ph, inner):
            part = ph // 2
            core = lax.rem(c + ph, 2)

            @pl.when((s > 0) & (s < 4) & (lax.rem(ph, 2) == 0))
            def _():
                ring_step_both(s, part)

            @pl.when((s > 0) & (s < 4) & (lax.rem(ph, 2) == 1))
            def _():
                sib_wait(part, N_Z - s)
                sib_wait(part, s)

            @pl.when((s == 4) & (ph == 0))
            def _():
                ring_step(s, 0, 0)
                ring_step(s, 1, 1)

            @pl.when(((s == 4) | (s == 0)) & (ph == 1))
            def _():
                sib_wait(0, s)
                sib_wait(1, s)

            @pl.when((s == 1) & (ph == 0))
            def _():
                for step in range(1, N_TENSOR):
                    w_copy(step).start()

            @pl.when((s == 3) & (ph == 3))
            def _():
                for step in range(1, N_TENSOR):
                    w_arrived(step)
                for j in range(N_TENSOR):
                    w_sib(j).start()

            side_x = lax.rem(h + part, 2)
            side_y = lax.rem(h + part + single, 2)
            attend(block_of(z + N_Z - s, side_x, core), block_of(z + s, side_y, core))
            return inner

        lax.fori_loop(0, 4 - 2 * single, phase, 0)
        return carry

    def ring_step_both(s, part):
        for p in range(2):

            @pl.when(part == p)
            def _():
                ring_step(s, p, 0)
                ring_step(s, p, 1)

    lax.fori_loop(0, 5, distance_step, 0)

    def finish(half):
        for i in range(4):
            rows = pl.ds(half * CAP + i * UNIT, UNIT)
            unit_live = jnp.sum(
                jnp.where(lane[:1, :] == half * 4 + i, query_live, 0.0), axis=1, keepdims=True
            )
            o = jnp.where(unit_live > 0.0, acc[rows, :HD] / acc[rows, HD:], 0.0)
            ob[half, pl.ds(i * UNIT, UNIT), :] = o.astype(jnp.bfloat16)

    def plane(dy, e_hi, e_lo):
        side = lax.rem(h + e_hi, 2)
        column = lax.rem(x_lo + e_lo, 2)
        return {"blk": block_of(z, side, c), "tensor": 2 * lax.rem(y + dy, 4) + column}

    def head_at(dy, e_hi, e_lo):
        return (
            4 * lax.rem(y + dy, 4) + 2 * lax.rem(x_lo + e_lo, 2) + lax.rem(h + e_hi, 2)
        )

    def send_head(src, dy, e_hi, e_lo, head, index):
        return remote(src, og.at[head], o_s.at[index], o_r.at[head], plane(dy, e_hi, e_lo))

    def send_transit(dy, index):
        return remote(ob.at[1], transit.at[dy - 1], o_s.at[index], t_r.at[dy - 1], plane(dy, 0, 0))

    def arrived(head):
        remote(ob.at[0], og.at[head], o_s.at[0], o_r.at[head], partner).wait_recv()

    def transit_arrived(dy):
        slot = transit.at[dy - 1]
        remote(slot, slot, o_s.at[0], t_r.at[dy - 1], partner).wait_recv()

    others = ((1, 0), (1, 1), (0, 1))
    steps = (1, 3, 2)

    finish(1)

    @pl.when(c == 0)
    def _():
        send_head(ob.at[1], 0, 1, 0, my_head, 0).start()
        send_head(ob.at[1], 0, 1, 1, my_head, 1).start()

    @pl.when(c == 1)
    def _():
        for i, dy in enumerate(steps):
            send_transit(dy, i).start()

    finish(0)

    @pl.when(c == 0)
    def _():
        send_head(ob.at[0], 0, 0, 1, my_head, 2).start()
        for i, dy in enumerate(steps):
            send_head(ob.at[0], dy, 0, 0, my_head, 3 + i).start()
        for k, (e_hi, e_lo) in enumerate(((0, 1), (1, 0), (1, 1))):
            head = head_at(0, e_hi, e_lo)
            arrived(head)
            for i, dy in enumerate(steps):
                send_head(og.at[head], dy, 0, 0, head, 6 + 3 * k + i).start()

    @pl.when(c == 1)
    def _():
        for i, dy in enumerate(steps):
            send_head(ob.at[0], dy, 0, 0, my_head, 3 + i).start()
        for i, (e_hi, e_lo) in enumerate(others):
            send_head(ob.at[e_hi], 0, e_hi, e_lo, my_head, 6 + i).start()
        for k, dy in enumerate(steps):
            transit_arrived(dy)
            head = head_at(4 - dy, 0, 0)
            send_head(transit.at[dy - 1], 0, 1, 0, head, 9 + 3 * k).start()
            send_head(transit.at[dy - 1], 0, 1, 1, head, 10 + 3 * k).start()
            arrived(head)
            send_head(og.at[head], 0, 0, 1, head, 11 + 3 * k).start()

    og[my_head] = ob[0]
    for j in range(N_TENSOR):
        w_sib_arrived(j)

    total[...] = jnp.zeros_like(total)
    for dy in (0, 1, 3, 2):
        for e_lo in range(2):
            first = 4 * lax.rem(y + dy, 4) + 2 * lax.rem(x_lo + e_lo, 2)

            for e_hi in range(2):
                head = head_at(dy, e_hi, e_lo)
                if dy > 0:
                    pl.when(c == 0)(functools.partial(arrived, head))
                if (e_hi, e_lo) != (0, 0):
                    pl.when(c == 1)(functools.partial(arrived, head))
            rows = jnp.concatenate([og[first], og[first + 1]], axis=1)
            weight = jnp.concatenate([wb[first], wb[first + 1]], axis=0)
            total[...] += jnp.dot(rows, weight, preferred_element_type=jnp.float32)
    out_ref[...] = total[...].astype(jnp.bfloat16)

    for copy in swaps:
        copy.wait_send()
    for step in range(1, N_TENSOR):
        w_copy(step).wait_send()
    for step in range(N_TENSOR):
        w_sib(step).wait_send()
    for index in range(15):
        send_head(ob.at[0], 1, 0, 0, my_head, index).wait_send()

    @pl.when(c == 1)
    def _():
        for index in range(15, 18):
            send_head(ob.at[0], 1, 0, 0, my_head, index).wait_send()

    def sent(index, carry):
        sib_copy(0, index).wait_send()
        return carry

    lax.fori_loop(0, 16, sent, 0)
    for part in range(2):
        for way in range(2):
            for step in range(4 if part == way else 3):
                ring_copy(0, part, way, step).wait_send()


def body(queries, key_states, value_states, out_weight, lengths, cycle_order):
    any_space = pl.BlockSpec(memory_space=pl.ANY)
    vmem = pl.BlockSpec(memory_space=pltpu.VMEM)
    dma = pltpu.SemaphoreType.DMA
    return pl.pallas_call(
        kernel,
        out_shape=jax.ShapeDtypeStruct((CAP, CAP), jnp.bfloat16),
        in_specs=[any_space] * 4 + [vmem] * 2,
        out_specs=vmem,
        scratch_shapes=[
            pltpu.VMEM((N_BLK, 2, CAP, HD), jnp.bfloat16),
            pltpu.VMEM((ROWS, 2 * HD), jnp.bfloat16),
            pltpu.VMEM((ROWS, 2 * HD), jnp.float32),
            pltpu.VMEM((ROWS, HD), jnp.float32),
            pltpu.VMEM((UNIT, 128), jnp.float32),
            pltpu.VMEM((2, CAP, HD), jnp.bfloat16),
            pltpu.VMEM((2 * N_TENSOR, CAP, HD), jnp.bfloat16),
            pltpu.VMEM((2 * N_TENSOR, HD, CAP), jnp.bfloat16),
            pltpu.VMEM((CAP, CAP), jnp.float32),
            pltpu.VMEM((3, CAP, HD), jnp.bfloat16),
            dma((4,)),
            dma((3,)),
            dma((3,)),
            dma((16,)),
            dma((16,)),
            dma((16,)),
            dma((16,)),
            dma((15,)),
            dma((15,)),
            dma((18,)),
            dma((16,)),
            dma((3,)),
        ],
        compiler_params=pltpu.CompilerParams(
            collective_id=0, has_side_effects=True, vmem_limit_bytes=56 * 2**20
        ),
        name="ring_attention",
    )(queries, key_states, value_states, out_weight, lengths.reshape(1, N_BLK), cycle_order.reshape(1, N_BLK))


def solution(mesh):
    placed = (
        P("blk", "tensor"),
        P("blk", "tensor"),
        P("blk", "tensor"),
        P("tensor", None),
        P(),
        P(),
    )
    return jax.shard_map(
        body, mesh=mesh, in_specs=placed, out_specs=P("blk", "tensor"), check_vma=False
    )
```

```python
import functools
import math

import jax
import jax.numpy as jnp
from jax import lax
from jax.experimental import pallas as pl
from jax.experimental.pallas import tpu as pltpu
from jax.sharding import PartitionSpec as P

HD = 128
UNIT = 128
CAP = 512
N_Z = 8
N_TENSOR = 8
N_BLK = 32
ROWS = 2 * CAP
TILE = 256
HALF = CAP // 2
NEG = -(2.0**100)
LOWEST = -(2.0**99)
EXP_SCALE = math.log2(math.e) / math.sqrt(HD)
MESH = pl.DeviceIdType.MESH
NT = (((1,), (1,)), ((), ()))


def block_of(z, h, c):
    return lax.rem(z, N_Z) * 4 + h * 2 + c


def kernel(
    q_ref, k_ref, v_ref, w_ref, len_ref, ord_ref, out_ref,
    kv, q2, acc, top, bias, ob, og, wb, total, transit,
    loc, par_s, par_r, ring_s, ring_r, sib_s, sib_r, w_s, w_r, o_s, o_r, t_r, hs_s, h_r,
):
    b = lax.axis_index("blk")
    t = lax.axis_index("tensor")
    z = b // 4
    h = lax.rem(b // 2, 2)
    c = lax.rem(b, 2)
    y = t // 2
    x_lo = lax.rem(t, 2)
    other_b = block_of(z, 1 - h, c)
    sibling = {"blk": block_of(z, h, 1 - c), "tensor": t}
    partner = {"blk": other_b, "tensor": t}
    z_up = {"blk": block_of(z + 1, h, c), "tensor": t}
    z_down = {"blk": block_of(z + N_Z - 1, h, c), "tensor": t}
    my_cols = pl.ds(pl.multiple_of(h * HD, HD), HD)
    other_cols = pl.ds(pl.multiple_of((1 - h) * HD, HD), HD)
    my_head = 2 * t + h

    def tensor_at(step):
        return lax.rem(t + step, N_TENSOR)

    def remote(src, dst, send, recv, device):
        return pltpu.make_async_remote_copy(
            src_ref=src, dst_ref=dst, send_sem=send, recv_sem=recv,
            device_id=device, device_id_type=MESH,
        )

    own = [
        pltpu.make_async_copy(k_ref.at[:, my_cols], kv.at[b, 0], loc.at[0]),
        pltpu.make_async_copy(v_ref.at[:, my_cols], kv.at[b, 1], loc.at[1]),
        pltpu.make_async_copy(q_ref.at[:, my_cols], q2.at[pl.ds(0, CAP), pl.ds(0, HD)], loc.at[2]),
        pltpu.make_async_copy(
            w_ref.at[
                pl.ds(pl.multiple_of(c * HD, HD), HD), pl.ds(pl.multiple_of(t * CAP, CAP), CAP)
            ],
            wb.at[2 * t + c],
            loc.at[3],
        ),
    ]
    for copy in own:
        copy.start()

    barrier = pltpu.get_barrier_semaphore()
    peers = [z_up, z_down, sibling]
    peers += [{"blk": b, "tensor": tensor_at(d)} for d in range(1, N_TENSOR)]
    peers += [{"blk": other_b, "tensor": 2 * y + side} for side in range(2)]
    for peer in peers:
        pl.semaphore_signal(barrier, inc=1, device_id=peer, device_id_type=MESH)

    lane = lax.broadcasted_iota(jnp.int32, (UNIT, 128), 1)
    row = lax.broadcasted_iota(jnp.int32, (UNIT, 128), 0)
    lengths = jnp.broadcast_to(len_ref[...].astype(jnp.float32), (UNIT, N_BLK))
    orders = jnp.broadcast_to(ord_ref[...].astype(jnp.float32), (UNIT, N_BLK))
    holder = lane[:, :N_BLK] == row[:, :N_BLK] // 4
    unit_start = (lax.rem(row[:, :1], 4) * UNIT).astype(jnp.float32)
    my_len = jnp.sum(jnp.where(holder, lengths, 0.0), axis=1, keepdims=True)
    my_order = jnp.sum(jnp.where(holder, orders, 0.0), axis=1, keepdims=True)
    before = jnp.where(orders < my_order, lengths, 0.0)
    position = jnp.sum(before, axis=1, keepdims=True) + unit_start
    is_live = unit_start < my_len
    query_unit = jnp.where(lane < 4, b * 4 + lane, other_b * 4 + lane - 4)
    chosen = (query_unit == row) & (lane < 8)
    query_position = jnp.sum(jnp.where(chosen, position, 0.0), axis=0, keepdims=True)
    query_live = jnp.sum(jnp.where(chosen & is_live, 1.0, 0.0), axis=0, keepdims=True)
    bias[...] = jnp.where(is_live & (position < query_position), 0.0, NEG)
    tile_row = lax.broadcasted_iota(jnp.int32, (ROWS, HD), 0) // UNIT
    tile_lane = lax.broadcasted_iota(jnp.int32, (ROWS, HD), 1)
    q2[:, HD:] = jnp.where(tile_row == tile_lane, 1.0, 0.0).astype(jnp.bfloat16)

    pl.semaphore_wait(barrier, len(peers))
    for copy in own:
        copy.wait()

    def piece(slot, half):
        return kv.at[slot, :, pl.ds(pl.multiple_of(half * HALF, HALF), HALF), :]

    def ring_copy(slot, part, half, way, step):
        index = part * 16 + half * 8 + way * 4 + step
        device = z_up if way == 0 else z_down
        at = piece(slot, half)
        return remote(at, at, ring_s.at[index], ring_r.at[index], device)

    def sib_copy(slot, part, half, distance):
        index = part * 16 + half * 8 + distance
        at = piece(slot, half)
        return remote(at, at, sib_s.at[index], sib_r.at[index], sibling)

    def swap(half, which):
        rows = pl.ds(half * HALF, HALF)
        index = half * 2 + which
        source = v_ref if which else k_ref
        return remote(
            source.at[rows, other_cols],
            kv.at[b, which, rows, :],
            par_s.at[index],
            par_r.at[index],
            partner,
        )

    def swapped(half, which):
        at = kv.at[other_b, which, pl.ds(half * HALF, HALF), :]
        index = half * 2 + which
        remote(at, at, par_s.at[index], par_r.at[index], partner).wait_recv()

    swap_q = remote(
        q_ref.at[:, other_cols],
        q2.at[pl.ds(CAP, CAP), pl.ds(0, HD)],
        par_s.at[4],
        par_r.at[4],
        partner,
    )

    def send_own(half):
        for way in range(2):
            ring_copy(b, 0, half, way, 0).start()
        for which in range(2):
            swap(half, which).start()
        sib_copy(b, 0, half, 0).start()

    def send_swapped(half):
        for which in range(2):
            swapped(half, which)
        for way in range(2):
            ring_copy(other_b, 1, half, way, 0).start()
        sib_copy(other_b, 1, half, 0).start()

    def ring_step(part, hop, half, way, onward):
        side = lax.rem(h + part, 2)
        distance = N_Z - hop if way == 0 else hop
        slot = block_of(z + distance, side, c)
        ring_copy(slot, part, half, way, hop - 1).wait_recv()
        if onward is not None:

            @pl.when(onward)
            def _():
                ring_copy(slot, part, half, way, hop).start()

        sib_copy(slot, part, half, distance).start()

    def event(part, hop, half):
        ring_step(part, hop, half, 0, hop < 3)
        ring_step(part, hop, half, 1, hop < 3 + part)

    def send_fourth():
        for half in range(2):
            ring_copy(block_of(z + N_Z - 3, h, c), 0, half, 0, 3).start()

    def last_event(half):
        ring_step(0, 4, half, 0, None)
        ring_step(1, 4, half, 1, None)

    swap_q.start()
    send_own(0)
    top[...] = jnp.full_like(top, LOWEST)
    acc[...] = jnp.zeros_like(acc)

    square_row = lax.broadcasted_iota(jnp.int32, (UNIT, UNIT), 0)
    square_lane = lax.broadcasted_iota(jnp.int32, (UNIT, UNIT), 1)

    def diagonal(slot, first):
        def unit(i, carry):
            rows = pl.ds(pl.multiple_of((first + i) * UNIT, UNIT), UNIT)
            keys = pl.ds(pl.multiple_of(i * UNIT, UNIT), UNIT)
            k = kv[slot, 0, keys, :]
            v = kv[slot, 1, keys, :]
            s = lax.dot_general(q2[rows, :HD], k, NT, preferred_element_type=jnp.float32)
            s = jnp.where(square_lane <= square_row, s, NEG)
            old = top[rows, :]
            best = jnp.maximum(old, jnp.max(s, axis=1, keepdims=True))
            shrink = jnp.exp2((old - best) * EXP_SCALE)
            p = jnp.exp2((s - best) * EXP_SCALE).astype(jnp.bfloat16)
            top[rows, :] = best
            acc[rows, :] = acc[rows, :] * jnp.concatenate([shrink, shrink], axis=1) + jnp.dot(
                p,
                jnp.concatenate([v, jnp.ones_like(v)], axis=1),
                preferred_element_type=jnp.float32,
            )
            return carry

        lax.fori_loop(0, 4, unit, 0)

    diagonal(b, 0)
    send_own(1)
    swap_q.wait_recv()
    event(0, 1, 0)

    def w_copy(step):
        target = tensor_at(step)
        return remote(
            w_ref.at[
                pl.ds(pl.multiple_of(c * HD, HD), HD), pl.ds(pl.multiple_of(target * CAP, CAP), CAP)
            ],
            wb.at[2 * t + c],
            w_s.at[step - 1],
            w_r.at[step - 1],
            {"blk": b, "tensor": target},
        )

    def w_arrived(step):
        source = tensor_at(N_TENSOR - step)
        slot = wb.at[2 * source + c]
        remote(slot, slot, w_s.at[step - 1], w_r.at[step - 1], sibling).wait_recv()

    def w_sib(j):
        slot = wb.at[2 * j + c]
        return remote(slot, slot, w_s.at[7 + j], w_r.at[7 + j], sibling)

    def w_sib_arrived(j):
        slot = wb.at[2 * j + 1 - c]
        remote(slot, slot, w_s.at[7 + j], w_r.at[7 + j], sibling).wait_recv()

    def attend(slot_x, slot_y, half=None):
        start, count = (0, CAP) if half is None else (pl.multiple_of(half * HALF, HALF), HALF)
        rows = pl.ds(start, count)
        keys = jnp.concatenate([kv[slot_x, 0, rows, :], kv[slot_y, 0, rows, :]], axis=0)
        values = jnp.concatenate([kv[slot_x, 1, rows, :], kv[slot_y, 1, rows, :]], axis=0)
        fills = []
        for slot in (slot_x, slot_y):
            first = slot * 4 if half is None else slot * 4 + half * 2
            for j in range(count // UNIT):
                fills.append(jnp.broadcast_to(bias[pl.ds(first + j, 1), :], (UNIT, HD)))
        keys = jnp.concatenate([keys, jnp.concatenate(fills, axis=0).astype(jnp.bfloat16)], axis=1)
        values = jnp.concatenate([values, jnp.ones_like(values)], axis=1)
        for i in range(ROWS // TILE):
            rows = pl.ds(i * TILE, TILE)
            s = lax.dot_general(q2[rows, :], keys, NT, preferred_element_type=jnp.float32)
            old = top[rows, :]
            best = jnp.maximum(old, jnp.max(s, axis=1, keepdims=True))
            shrink = jnp.exp2((old - best) * EXP_SCALE)
            top[rows, :] = best
            p = jnp.concatenate(
                [
                    jnp.exp2((s[:, j * 128 : (j + 1) * 128] - best) * EXP_SCALE).astype(
                        jnp.bfloat16
                    )
                    for j in range(s.shape[1] // 128)
                ],
                axis=1,
            )
            update = jnp.dot(p, values, preferred_element_type=jnp.float32)
            acc[rows, :] = acc[rows, :] * jnp.concatenate([shrink, shrink], axis=1) + update

    def sib_wait(part, half, distance):
        side = lax.rem(h + part, 2)
        slot = block_of(z + distance, side, 1 - c)
        sib_copy(slot, part, half, distance).wait_recv()

    for half in range(2):
        sib_wait(0, half, 0)
    attend(b, block_of(z, h, 1 - c))

    def round_step(r, carry):
        part = 1 - lax.rem(r, 2)
        s = (r + 1) // 2 - part
        single = (4 - s) // 4

        def phase(ph, inner):
            core = lax.rem(c + ph, 2)

            @pl.when((ph == 0) & ((r == 1) | (r > 3)))
            def _():
                event(part, s, 1)

            @pl.when((ph == 0) & (r == 1))
            def _():
                send_swapped(0)

            @pl.when((ph == 1) & (r == 1))
            def _():
                send_swapped(1)
                event(0, 2, 0)

            @pl.when(r == 2)
            def _():
                event(0, 2, 1)
                for step in range(1, N_TENSOR):
                    w_copy(step).start()
                diagonal(other_b, 4)
                for half in range(2):
                    sib_wait(1, half, 0)

            @pl.when((ph == 0) & (r == 6))
            def _():
                send_fourth()

            @pl.when((ph == 1) & (r > 2) & (r < 6))
            def _():
                following = 1 - part
                event(following, (r + 2) // 2 - following, 0)

            @pl.when((ph == 1) & (r == 6))
            def _():
                event(1, 3, 0)
                for step in range(1, N_TENSOR):
                    w_arrived(step)
                for j in range(N_TENSOR):
                    w_sib(j).start()

            @pl.when((ph == 1) & (r == 8))
            def _():
                last_event(0)

            @pl.when(ph == 1)
            def _():
                for half in range(2):
                    sib_wait(part, half, N_Z - s)
                    sib_wait(part, half, s)

            side = lax.rem(h + part, 2)
            core_y = lax.rem(core + single, 2)
            attend(block_of(z + N_Z - s, side, core), block_of(z + s, side, core_y))
            return inner

        lax.fori_loop(0, 2 - single - 2 * (s // 4), phase, 0)
        return carry

    lax.fori_loop(1, 9, round_step, 0)

    def last_step(i, carry):
        half = i // 2
        core = lax.rem(c + i, 2)

        @pl.when(i == 2)
        def _():
            last_event(1)

        @pl.when(lax.rem(i, 2) == 1)
        def _():
            sib_wait(0, half, 4)
            sib_wait(1, half, 4)

        attend(block_of(z + 4, h, core), block_of(z + 4, 1 - h, core), half)
        return carry

    lax.fori_loop(0, 4, last_step, 0)

    def finish(half):
        for i in range(4):
            rows = pl.ds(half * CAP + i * UNIT, UNIT)
            unit_live = jnp.sum(
                jnp.where(lane[:1, :] == half * 4 + i, query_live, 0.0), axis=1, keepdims=True
            )
            o = jnp.where(unit_live > 0.0, acc[rows, :HD] / acc[rows, HD:], 0.0)
            ob[half, pl.ds(i * UNIT, UNIT), :] = o.astype(jnp.bfloat16)

    def plane(dy, e_hi, e_lo):
        side = lax.rem(h + e_hi, 2)
        column = lax.rem(x_lo + e_lo, 2)
        return {"blk": block_of(z, side, c), "tensor": 2 * lax.rem(y + dy, 4) + column}

    def head_at(dy, e_hi, e_lo):
        return (
            4 * lax.rem(y + dy, 4) + 2 * lax.rem(x_lo + e_lo, 2) + lax.rem(h + e_hi, 2)
        )

    def send_head(src, dy, e_hi, e_lo, head, index):
        return remote(src, og.at[head], o_s.at[index], o_r.at[head], plane(dy, e_hi, e_lo))

    def send_transit(dy, index):
        return remote(ob.at[1], transit.at[dy - 1], o_s.at[index], t_r.at[dy - 1], plane(dy, 0, 0))

    def arrived(head):
        remote(ob.at[0], og.at[head], o_s.at[0], o_r.at[head], partner).wait_recv()

    def transit_arrived(dy):
        slot = transit.at[dy - 1]
        remote(slot, slot, o_s.at[0], t_r.at[dy - 1], partner).wait_recv()

    def send_half(half, dy, head, index):
        at = og.at[head, pl.ds(half * HALF, HALF), :]
        return remote(at, at, hs_s.at[index], h_r.at[half * 16 + head], plane(dy, 0, 0))

    def half_arrived(half, head):
        at = og.at[head, pl.ds(half * HALF, HALF), :]
        remote(at, at, hs_s.at[0], h_r.at[half * 16 + head], partner).wait_recv()

    others = ((1, 0), (1, 1), (0, 1))
    steps = (1, 3, 2)

    finish(1)

    @pl.when(c == 0)
    def _():
        send_head(ob.at[1], 0, 1, 0, my_head, 0).start()
        send_head(ob.at[1], 0, 1, 1, my_head, 1).start()

    @pl.when(c == 1)
    def _():
        for i, dy in enumerate(steps):
            send_transit(dy, i).start()

    finish(0)

    @pl.when(c == 0)
    def _():
        send_head(ob.at[0], 0, 0, 1, my_head, 2).start()
        for i, dy in enumerate((1, 3)):
            send_head(ob.at[0], dy, 0, 0, my_head, 3 + i).start()
        lanes = ((0, 0), (0, 1), (1, 1), (1, 0))
        for k, (e_hi, e_lo) in enumerate(lanes):
            if k > 0:
                head = head_at(0, e_hi, e_lo)
                arrived(head)
                for i, dy in enumerate((1, 3)):
                    send_head(og.at[head], dy, 0, 0, head, 3 + 2 * k + i).start()
        for k, (e_hi, e_lo) in enumerate(lanes):
            for i, dy in enumerate((1, 3)):
                head = head_at(4 - dy, e_hi, e_lo)
                arrived(head)
                send_half(i, dy, head, 2 * k + i).start()

    @pl.when(c == 1)
    def _():
        for i, dy in enumerate(steps):
            send_head(ob.at[0], dy, 0, 0, my_head, 3 + i).start()
        for i, (e_hi, e_lo) in enumerate(others):
            send_head(ob.at[e_hi], 0, e_hi, e_lo, my_head, 6 + i).start()
        for k, dy in enumerate(steps):
            transit_arrived(dy)
            head = head_at(4 - dy, 0, 0)
            send_head(transit.at[dy - 1], 0, 1, 0, head, 9 + 3 * k).start()
            send_head(transit.at[dy - 1], 0, 1, 1, head, 10 + 3 * k).start()
            arrived(head)
            send_head(og.at[head], 0, 0, 1, head, 11 + 3 * k).start()

    og[my_head] = ob[0]
    for j in range(N_TENSOR):
        w_sib_arrived(j)

    total[...] = jnp.zeros_like(total)
    for dy in (0, 1, 3, 2):
        for e_lo in range(2):
            first = 4 * lax.rem(y + dy, 4) + 2 * lax.rem(x_lo + e_lo, 2)

            for e_hi in range(2):
                head = head_at(dy, e_hi, e_lo)
                if dy == 2:
                    pl.when(c == 0)(functools.partial(half_arrived, 0, head))
                    pl.when(c == 0)(functools.partial(half_arrived, 1, head))
                if (e_hi, e_lo) != (0, 0):
                    pl.when(c == 1)(functools.partial(arrived, head))
            rows = jnp.concatenate([og[first], og[first + 1]], axis=1)
            weight = jnp.concatenate([wb[first], wb[first + 1]], axis=0)
            total[...] += jnp.dot(rows, weight, preferred_element_type=jnp.float32)
    out_ref[...] = total[...].astype(jnp.bfloat16)

    for half in range(2):
        for which in range(2):
            swap(half, which).wait_send()
    swap_q.wait_send()
    for step in range(1, N_TENSOR):
        w_copy(step).wait_send()
    for step in range(N_TENSOR):
        w_sib(step).wait_send()

    def head_sent(index, carry):
        send_head(ob.at[0], 1, 0, 0, my_head, index).wait_send()
        return carry

    def relay_sent(index, carry):
        send_half(0, 1, my_head, index).wait_send()
        return carry

    lax.fori_loop(0, 11 + 7 * c, head_sent, 0)
    lax.fori_loop(0, 8 * (1 - c), relay_sent, 0)

    def sent(i, carry):
        part = i // 2
        half = lax.rem(i, 2)

        def sib_sent(distance, inner):
            sib_copy(0, part, half, distance).wait_send()
            return inner

        lax.fori_loop(0, N_Z, sib_sent, 0)
        for way in range(2):

            def ring_sent(step, inner, way=way):
                ring_copy(0, part, half, way, step).wait_send()
                return inner

            reach = 4 - part if way == 0 else 3 + part
            lax.fori_loop(0, reach, ring_sent, 0)
        return carry

    lax.fori_loop(0, 4, sent, 0)


def body(queries, key_states, value_states, out_weight, lengths, cycle_order):
    any_space = pl.BlockSpec(memory_space=pl.ANY)
    vmem = pl.BlockSpec(memory_space=pltpu.VMEM)
    dma = pltpu.SemaphoreType.DMA
    return pl.pallas_call(
        kernel,
        out_shape=jax.ShapeDtypeStruct((CAP, CAP), jnp.bfloat16),
        in_specs=[any_space] * 4 + [vmem] * 2,
        out_specs=vmem,
        scratch_shapes=[
            pltpu.VMEM((N_BLK, 2, CAP, HD), jnp.bfloat16),
            pltpu.VMEM((ROWS, 2 * HD), jnp.bfloat16),
            pltpu.VMEM((ROWS, 2 * HD), jnp.float32),
            pltpu.VMEM((ROWS, HD), jnp.float32),
            pltpu.VMEM((UNIT, 128), jnp.float32),
            pltpu.VMEM((2, CAP, HD), jnp.bfloat16),
            pltpu.VMEM((2 * N_TENSOR, CAP, HD), jnp.bfloat16),
            pltpu.VMEM((2 * N_TENSOR, HD, CAP), jnp.bfloat16),
            pltpu.VMEM((CAP, CAP), jnp.float32),
            pltpu.VMEM((3, CAP, HD), jnp.bfloat16),
            dma((4,)),
            dma((5,)),
            dma((5,)),
            dma((32,)),
            dma((32,)),
            dma((32,)),
            dma((32,)),
            dma((15,)),
            dma((15,)),
            dma((18,)),
            dma((16,)),
            dma((3,)),
            dma((8,)),
            dma((32,)),
        ],
        compiler_params=pltpu.CompilerParams(
            collective_id=0, has_side_effects=True, vmem_limit_bytes=56 * 2**20
        ),
        name="ring_attention",
    )(queries, key_states, value_states, out_weight, lengths.reshape(1, N_BLK), cycle_order.reshape(1, N_BLK))


def solution(mesh):
    placed = (
        P("blk", "tensor"),
        P("blk", "tensor"),
        P("blk", "tensor"),
        P("tensor", None),
        P(),
        P(),
    )
    return jax.shard_map(
        body, mesh=mesh, in_specs=placed, out_specs=P("blk", "tensor"), check_vma=False
    )
```

```python
import functools
import math

import jax
import jax.numpy as jnp
from jax import lax
from jax.experimental import pallas as pl
from jax.experimental.pallas import tpu as pltpu
from jax.sharding import PartitionSpec as P

HD = 128
UNIT = 128
CAP = 512
N_Z = 8
N_TENSOR = 8
N_BLK = 32
ROWS = 2 * CAP
TILE = 256
HALF = CAP // 2
NEG = -(2.0**100)
LOWEST = -(2.0**99)
EXP_SCALE = math.log2(math.e) / math.sqrt(HD)
MESH = pl.DeviceIdType.MESH
NT = (((1,), (1,)), ((), ()))


def block_of(z, h, c):
    return lax.rem(z, N_Z) * 4 + h * 2 + c


def kernel(
    q_ref, k_ref, v_ref, w_ref, len_ref, ord_ref, out_ref,
    kv, q2, acc, top, bias, ob, og, wb, total, transit,
    loc, par_s, par_r, ring_s, ring_r, sib_s, sib_r, w_s, w_r, o_s, o_r, t_r, hs_s, h_r,
):
    b = lax.axis_index("blk")
    t = lax.axis_index("tensor")
    z = b // 4
    h = lax.rem(b // 2, 2)
    c = lax.rem(b, 2)
    y = t // 2
    x_lo = lax.rem(t, 2)
    other_b = block_of(z, 1 - h, c)
    sibling = {"blk": block_of(z, h, 1 - c), "tensor": t}
    partner = {"blk": other_b, "tensor": t}
    z_up = {"blk": block_of(z + 1, h, c), "tensor": t}
    z_down = {"blk": block_of(z + N_Z - 1, h, c), "tensor": t}
    my_cols = pl.ds(pl.multiple_of(h * HD, HD), HD)
    other_cols = pl.ds(pl.multiple_of((1 - h) * HD, HD), HD)
    my_head = 2 * t + h

    def tensor_at(step):
        return lax.rem(t + step, N_TENSOR)

    def remote(src, dst, send, recv, device):
        return pltpu.make_async_remote_copy(
            src_ref=src, dst_ref=dst, send_sem=send, recv_sem=recv,
            device_id=device, device_id_type=MESH,
        )

    own = [
        pltpu.make_async_copy(k_ref.at[:, my_cols], kv.at[b, 0], loc.at[0]),
        pltpu.make_async_copy(v_ref.at[:, my_cols], kv.at[b, 1], loc.at[1]),
        pltpu.make_async_copy(q_ref.at[:, my_cols], q2.at[pl.ds(0, CAP), pl.ds(0, HD)], loc.at[2]),
        pltpu.make_async_copy(
            w_ref.at[
                pl.ds(pl.multiple_of(c * HD, HD), HD), pl.ds(pl.multiple_of(t * CAP, CAP), CAP)
            ],
            wb.at[2 * t + c],
            loc.at[3],
        ),
    ]
    for copy in own:
        copy.start()

    barrier = pltpu.get_barrier_semaphore()
    peers = [z_up, z_down, sibling]
    peers += [{"blk": b, "tensor": tensor_at(d)} for d in range(1, N_TENSOR)]
    peers += [{"blk": other_b, "tensor": 2 * y + side} for side in range(2)]
    for peer in peers:
        pl.semaphore_signal(barrier, inc=1, device_id=peer, device_id_type=MESH)

    lane = lax.broadcasted_iota(jnp.int32, (UNIT, 128), 1)
    row = lax.broadcasted_iota(jnp.int32, (UNIT, 128), 0)
    lengths = jnp.broadcast_to(len_ref[...].astype(jnp.float32), (UNIT, N_BLK))
    orders = jnp.broadcast_to(ord_ref[...].astype(jnp.float32), (UNIT, N_BLK))
    holder = lane[:, :N_BLK] == row[:, :N_BLK] // 4
    unit_start = (lax.rem(row[:, :1], 4) * UNIT).astype(jnp.float32)
    my_len = jnp.sum(jnp.where(holder, lengths, 0.0), axis=1, keepdims=True)
    my_order = jnp.sum(jnp.where(holder, orders, 0.0), axis=1, keepdims=True)
    before = jnp.where(orders < my_order, lengths, 0.0)
    position = jnp.sum(before, axis=1, keepdims=True) + unit_start
    is_live = unit_start < my_len
    query_unit = jnp.where(lane < 4, b * 4 + lane, other_b * 4 + lane - 4)
    chosen = (query_unit == row) & (lane < 8)
    query_position = jnp.sum(jnp.where(chosen, position, 0.0), axis=0, keepdims=True)
    query_live = jnp.sum(jnp.where(chosen & is_live, 1.0, 0.0), axis=0, keepdims=True)
    bias[...] = jnp.where(is_live & (position < query_position), 0.0, NEG)
    tile_row = lax.broadcasted_iota(jnp.int32, (ROWS, HD), 0) // UNIT
    tile_lane = lax.broadcasted_iota(jnp.int32, (ROWS, HD), 1)
    q2[:, HD:] = jnp.where(tile_row == tile_lane, 1.0, 0.0).astype(jnp.bfloat16)

    pl.semaphore_wait(barrier, len(peers))
    for copy in own:
        copy.wait()

    def piece(slot, half):
        return kv.at[slot, :, pl.ds(pl.multiple_of(half * HALF, HALF), HALF), :]

    def ring_copy(slot, part, half, way, step):
        index = part * 16 + half * 8 + way * 4 + step
        device = z_up if way == 0 else z_down
        at = piece(slot, half)
        return remote(at, at, ring_s.at[index], ring_r.at[index], device)

    def sib_copy(slot, part, half, distance):
        index = part * 16 + half * 8 + distance
        at = piece(slot, half)
        return remote(at, at, sib_s.at[index], sib_r.at[index], sibling)

    def swap(half, which):
        rows = pl.ds(half * HALF, HALF)
        index = half * 2 + which
        source = v_ref if which else k_ref
        return remote(
            source.at[rows, other_cols],
            kv.at[b, which, rows, :],
            par_s.at[index],
            par_r.at[index],
            partner,
        )

    def swapped(half, which):
        at = kv.at[other_b, which, pl.ds(half * HALF, HALF), :]
        index = half * 2 + which
        remote(at, at, par_s.at[index], par_r.at[index], partner).wait_recv()

    swap_q = remote(
        q_ref.at[:, other_cols],
        q2.at[pl.ds(CAP, CAP), pl.ds(0, HD)],
        par_s.at[4],
        par_r.at[4],
        partner,
    )

    def send_own(half):
        for way in range(2):
            ring_copy(b, 0, half, way, 0).start()
        sib_copy(b, 0, half, 0).start()

    def send_swap(half):
        for which in range(2):
            swap(half, which).start()

    def send_swapped(half):
        for which in range(2):
            swapped(half, which)
        for way in range(2):
            ring_copy(other_b, 1, half, way, 0).start()
        sib_copy(other_b, 1, half, 0).start()

    def ring_step(part, hop, half, way, onward):
        side = lax.rem(h + part, 2)
        distance = N_Z - hop if way == 0 else hop
        slot = block_of(z + distance, side, c)
        ring_copy(slot, part, half, way, hop - 1).wait_recv()
        if onward is not None:

            @pl.when(onward)
            def _():
                ring_copy(slot, part, half, way, hop).start()

        sib_copy(slot, part, half, distance).start()

    def event(part, hop, half):
        ring_step(part, hop, half, 0, hop < 3)
        ring_step(part, hop, half, 1, hop < 3 + part)

    def send_fourth():
        for half in range(2):
            ring_copy(block_of(z + N_Z - 3, h, c), 0, half, 0, 3).start()

    def last_event(half):
        ring_step(0, 4, half, 0, None)
        ring_step(1, 4, half, 1, None)

    swap_q.start()
    send_own(0)
    top[...] = jnp.full_like(top, LOWEST)
    acc[...] = jnp.zeros_like(acc)

    square_row = lax.broadcasted_iota(jnp.int32, (UNIT, UNIT), 0)
    square_lane = lax.broadcasted_iota(jnp.int32, (UNIT, UNIT), 1)

    def diagonal(slot, first):
        def unit(i, carry):
            rows = pl.ds(pl.multiple_of((first + i) * UNIT, UNIT), UNIT)
            keys = pl.ds(pl.multiple_of(i * UNIT, UNIT), UNIT)
            k = kv[slot, 0, keys, :]
            v = kv[slot, 1, keys, :]
            s = lax.dot_general(q2[rows, :HD], k, NT, preferred_element_type=jnp.float32)
            s = jnp.where(square_lane <= square_row, s, NEG)
            old = top[rows, :]
            best = jnp.maximum(old, jnp.max(s, axis=1, keepdims=True))
            shrink = jnp.exp2((old - best) * EXP_SCALE)
            p = jnp.exp2((s - best) * EXP_SCALE).astype(jnp.bfloat16)
            top[rows, :] = best
            acc[rows, :] = acc[rows, :] * jnp.concatenate([shrink, shrink], axis=1) + jnp.dot(
                p,
                jnp.concatenate([v, jnp.ones_like(v)], axis=1),
                preferred_element_type=jnp.float32,
            )
            return carry

        lax.fori_loop(0, 4, unit, 0, unroll=True)

    diagonal(b, 0)
    send_swap(0)
    send_own(1)
    swap_q.wait_recv()
    send_swap(1)
    event(0, 1, 0)

    def w_copy(step):
        target = tensor_at(step)
        return remote(
            w_ref.at[
                pl.ds(pl.multiple_of(c * HD, HD), HD), pl.ds(pl.multiple_of(target * CAP, CAP), CAP)
            ],
            wb.at[2 * t + c],
            w_s.at[step - 1],
            w_r.at[step - 1],
            {"blk": b, "tensor": target},
        )

    def w_arrived(step):
        source = tensor_at(N_TENSOR - step)
        slot = wb.at[2 * source + c]
        remote(slot, slot, w_s.at[step - 1], w_r.at[step - 1], sibling).wait_recv()

    def w_sib(j):
        slot = wb.at[2 * j + c]
        return remote(slot, slot, w_s.at[7 + j], w_r.at[7 + j], sibling)

    def w_sib_arrived(j):
        slot = wb.at[2 * j + 1 - c]
        remote(slot, slot, w_s.at[7 + j], w_r.at[7 + j], sibling).wait_recv()

    def attend(slot_x, slot_y, half=None):
        start, count = (0, CAP) if half is None else (pl.multiple_of(half * HALF, HALF), HALF)
        rows = pl.ds(start, count)
        keys = jnp.concatenate([kv[slot_x, 0, rows, :], kv[slot_y, 0, rows, :]], axis=0)
        values = jnp.concatenate([kv[slot_x, 1, rows, :], kv[slot_y, 1, rows, :]], axis=0)
        fills = []
        for slot in (slot_x, slot_y):
            first = slot * 4 if half is None else slot * 4 + half * 2
            for j in range(count // UNIT):
                fills.append(jnp.broadcast_to(bias[pl.ds(first + j, 1), :], (UNIT, HD)))
        keys = jnp.concatenate([keys, jnp.concatenate(fills, axis=0).astype(jnp.bfloat16)], axis=1)
        values = jnp.concatenate([values, jnp.ones_like(values)], axis=1)
        for i in range(ROWS // TILE):
            rows = pl.ds(i * TILE, TILE)
            s = lax.dot_general(q2[rows, :], keys, NT, preferred_element_type=jnp.float32)
            old = top[rows, :]
            best = jnp.maximum(old, jnp.max(s, axis=1, keepdims=True))
            shrink = jnp.exp2((old - best) * EXP_SCALE)
            top[rows, :] = best
            p = jnp.concatenate(
                [
                    jnp.exp2((s[:, j * 128 : (j + 1) * 128] - best) * EXP_SCALE).astype(
                        jnp.bfloat16
                    )
                    for j in range(s.shape[1] // 128)
                ],
                axis=1,
            )
            update = jnp.dot(p, values, preferred_element_type=jnp.float32)
            acc[rows, :] = acc[rows, :] * jnp.concatenate([shrink, shrink], axis=1) + update

    def sib_wait(part, half, distance):
        side = lax.rem(h + part, 2)
        slot = block_of(z + distance, side, 1 - c)
        sib_copy(slot, part, half, distance).wait_recv()

    for half in range(2):
        sib_wait(0, half, 0)
    attend(b, block_of(z, h, 1 - c))

    def round_step(r, carry):
        part = 1 - lax.rem(r, 2)
        s = (r + 1) // 2 - part
        single = (4 - s) // 4

        def phase(ph, inner):
            core = lax.rem(c + ph, 2)

            @pl.when((ph == 0) & ((r == 1) | (r > 3)))
            def _():
                event(part, s, 1)

            @pl.when((ph == 0) & (r == 1))
            def _():
                send_swapped(0)

            @pl.when((ph == 1) & (r == 1))
            def _():
                send_swapped(1)
                event(0, 2, 0)

            @pl.when(r == 2)
            def _():
                event(0, 2, 1)
                for step in range(1, N_TENSOR):
                    w_copy(step).start()
                diagonal(other_b, 4)
                for half in range(2):
                    sib_wait(1, half, 0)

            @pl.when((ph == 0) & (r == 6))
            def _():
                send_fourth()

            @pl.when((ph == 1) & (r > 2) & (r < 6))
            def _():
                following = 1 - part
                event(following, (r + 2) // 2 - following, 0)

            @pl.when((ph == 1) & (r == 6))
            def _():
                event(1, 3, 0)
                for step in range(1, N_TENSOR):
                    w_arrived(step)
                for j in range(N_TENSOR):
                    w_sib(j).start()

            @pl.when((ph == 1) & (r == 8))
            def _():
                last_event(0)

            @pl.when(ph == 1)
            def _():
                for half in range(2):
                    sib_wait(part, half, N_Z - s)
                    sib_wait(part, half, s)

            side = lax.rem(h + part, 2)
            core_y = lax.rem(core + single, 2)
            attend(block_of(z + N_Z - s, side, core), block_of(z + s, side, core_y))
            return inner

        lax.fori_loop(0, 2 - single - 2 * (s // 4), phase, 0)
        return carry

    lax.fori_loop(1, 9, round_step, 0)

    def last_step(i, carry):
        half = i // 2
        core = lax.rem(c + i, 2)

        @pl.when(i == 2)
        def _():
            last_event(1)

        @pl.when(lax.rem(i, 2) == 1)
        def _():
            sib_wait(0, half, 4)
            sib_wait(1, half, 4)

        attend(block_of(z + 4, h, core), block_of(z + 4, 1 - h, core), half)
        return carry

    lax.fori_loop(0, 4, last_step, 0)

    def finish(half):
        for i in range(4):
            rows = pl.ds(half * CAP + i * UNIT, UNIT)
            unit_live = jnp.sum(
                jnp.where(lane[:1, :] == half * 4 + i, query_live, 0.0), axis=1, keepdims=True
            )
            o = jnp.where(unit_live > 0.0, acc[rows, :HD] / acc[rows, HD:], 0.0)
            ob[half, pl.ds(i * UNIT, UNIT), :] = o.astype(jnp.bfloat16)

    def plane(dy, e_hi, e_lo):
        side = lax.rem(h + e_hi, 2)
        column = lax.rem(x_lo + e_lo, 2)
        return {"blk": block_of(z, side, c), "tensor": 2 * lax.rem(y + dy, 4) + column}

    def head_at(dy, e_hi, e_lo):
        return (
            4 * lax.rem(y + dy, 4) + 2 * lax.rem(x_lo + e_lo, 2) + lax.rem(h + e_hi, 2)
        )

    def send_head(src, dy, e_hi, e_lo, head, index):
        return remote(src, og.at[head], o_s.at[index], o_r.at[head], plane(dy, e_hi, e_lo))

    def send_transit(dy, index):
        return remote(ob.at[1], transit.at[dy - 1], o_s.at[index], t_r.at[dy - 1], plane(dy, 0, 0))

    def arrived(head):
        remote(ob.at[0], og.at[head], o_s.at[0], o_r.at[head], partner).wait_recv()

    def transit_arrived(dy):
        slot = transit.at[dy - 1]
        remote(slot, slot, o_s.at[0], t_r.at[dy - 1], partner).wait_recv()

    def send_half(half, dy, head, index):
        at = og.at[head, pl.ds(half * HALF, HALF), :]
        return remote(at, at, hs_s.at[index], h_r.at[half * 16 + head], plane(dy, 0, 0))

    def half_arrived(half, head):
        at = og.at[head, pl.ds(half * HALF, HALF), :]
        remote(at, at, hs_s.at[0], h_r.at[half * 16 + head], partner).wait_recv()

    others = ((1, 0), (1, 1), (0, 1))
    steps = (1, 3, 2)

    finish(1)

    @pl.when(c == 0)
    def _():
        send_head(ob.at[1], 0, 1, 0, my_head, 0).start()
        send_head(ob.at[1], 0, 1, 1, my_head, 1).start()

    @pl.when(c == 1)
    def _():
        for i, dy in enumerate(steps):
            send_transit(dy, i).start()

    finish(0)

    @pl.when(c == 0)
    def _():
        send_head(ob.at[0], 0, 0, 1, my_head, 2).start()
        for i, dy in enumerate((1, 3)):
            send_head(ob.at[0], dy, 0, 0, my_head, 3 + i).start()

    @pl.when(c == 1)
    def _():
        for i, dy in enumerate(steps):
            send_head(ob.at[0], dy, 0, 0, my_head, 3 + i).start()
        for i, (e_hi, e_lo) in enumerate(others):
            send_head(ob.at[e_hi], 0, e_hi, e_lo, my_head, 6 + i).start()

    og[my_head] = ob[0]
    for j in range(N_TENSOR):
        w_sib_arrived(j)

    for half in range(2):
        for which in range(2):
            swap(half, which).wait_send()
    swap_q.wait_send()
    for step in range(1, N_TENSOR):
        w_copy(step).wait_send()
    for step in range(N_TENSOR):
        w_sib(step).wait_send()

    def sent(i, carry):
        part = i // 2
        half = lax.rem(i, 2)

        def sib_sent(distance, inner):
            sib_copy(0, part, half, distance).wait_send()
            return inner

        lax.fori_loop(0, N_Z, sib_sent, 0)
        for way in range(2):

            def ring_sent(step, inner, way=way):
                ring_copy(0, part, half, way, step).wait_send()
                return inner

            reach = 4 - part if way == 0 else 3 + part
            lax.fori_loop(0, reach, ring_sent, 0)
        return carry

    lax.fori_loop(0, 4, sent, 0)

    @pl.when(c == 0)
    def _():
        lanes = ((0, 0), (0, 1), (1, 1), (1, 0))
        for k, (e_hi, e_lo) in enumerate(lanes):
            if k > 0:
                head = head_at(0, e_hi, e_lo)
                arrived(head)
                for i, dy in enumerate((1, 3)):
                    send_head(og.at[head], dy, 0, 0, head, 3 + 2 * k + i).start()
        for k, (e_hi, e_lo) in enumerate(lanes):
            for i, dy in enumerate((1, 3)):
                head = head_at(4 - dy, e_hi, e_lo)
                arrived(head)
                send_half(i, dy, head, 2 * k + i).start()

    @pl.when(c == 1)
    def _():
        for k, dy in enumerate(steps):
            transit_arrived(dy)
            head = head_at(4 - dy, 0, 0)
            send_head(transit.at[dy - 1], 0, 1, 0, head, 9 + 3 * k).start()
            send_head(transit.at[dy - 1], 0, 1, 1, head, 10 + 3 * k).start()
            arrived(head)
            send_head(og.at[head], 0, 0, 1, head, 11 + 3 * k).start()

    for dy in (0, 1, 3, 2):
        for e_lo in range(2):
            first = 4 * lax.rem(y + dy, 4) + 2 * lax.rem(x_lo + e_lo, 2)

            for e_hi in range(2):
                head = head_at(dy, e_hi, e_lo)
                if dy == 2:
                    pl.when(c == 0)(functools.partial(half_arrived, 0, head))
                    pl.when(c == 0)(functools.partial(half_arrived, 1, head))
                if (e_hi, e_lo) != (0, 0):
                    pl.when(c == 1)(functools.partial(arrived, head))
            rows = jnp.concatenate([og[first], og[first + 1]], axis=1)
            weight = jnp.concatenate([wb[first], wb[first + 1]], axis=0)
            product = jnp.dot(rows, weight, preferred_element_type=jnp.float32)
            if (dy, e_lo) == (0, 0):
                total[...] = product
            elif (dy, e_lo) == (2, 1):
                out_ref[...] = (total[...] + product).astype(jnp.bfloat16)
            else:
                total[...] += product

    def head_sent(index, carry):
        send_head(ob.at[0], 1, 0, 0, my_head, index).wait_send()
        return carry

    def relay_sent(index, carry):
        send_half(0, 1, my_head, index).wait_send()
        return carry

    lax.fori_loop(0, 11 + 7 * c, head_sent, 0)
    lax.fori_loop(0, 8 * (1 - c), relay_sent, 0)


def body(queries, key_states, value_states, out_weight, lengths, cycle_order):
    any_space = pl.BlockSpec(memory_space=pl.ANY)
    vmem = pl.BlockSpec(memory_space=pltpu.VMEM)
    dma = pltpu.SemaphoreType.DMA
    return pl.pallas_call(
        kernel,
        out_shape=jax.ShapeDtypeStruct((CAP, CAP), jnp.bfloat16),
        in_specs=[any_space] * 4 + [vmem] * 2,
        out_specs=vmem,
        scratch_shapes=[
            pltpu.VMEM((N_BLK, 2, CAP, HD), jnp.bfloat16),
            pltpu.VMEM((ROWS, 2 * HD), jnp.bfloat16),
            pltpu.VMEM((ROWS, 2 * HD), jnp.float32),
            pltpu.VMEM((ROWS, HD), jnp.float32),
            pltpu.VMEM((UNIT, 128), jnp.float32),
            pltpu.VMEM((2, CAP, HD), jnp.bfloat16),
            pltpu.VMEM((2 * N_TENSOR, CAP, HD), jnp.bfloat16),
            pltpu.VMEM((2 * N_TENSOR, HD, CAP), jnp.bfloat16),
            pltpu.VMEM((CAP, CAP), jnp.float32),
            pltpu.VMEM((3, CAP, HD), jnp.bfloat16),
            dma((4,)),
            dma((5,)),
            dma((5,)),
            dma((32,)),
            dma((32,)),
            dma((32,)),
            dma((32,)),
            dma((15,)),
            dma((15,)),
            dma((18,)),
            dma((16,)),
            dma((3,)),
            dma((8,)),
            dma((32,)),
        ],
        compiler_params=pltpu.CompilerParams(
            collective_id=0, has_side_effects=True, vmem_limit_bytes=56 * 2**20
        ),
        name="ring_attention",
    )(queries, key_states, value_states, out_weight, lengths.reshape(1, N_BLK), cycle_order.reshape(1, N_BLK))


def solution(mesh):
    placed = (
        P("blk", "tensor"),
        P("blk", "tensor"),
        P("blk", "tensor"),
        P("tensor", None),
        P(),
        P(),
    )
    return jax.shard_map(
        body, mesh=mesh, in_specs=placed, out_specs=P("blk", "tensor"), check_vma=False
    )
```

```python
import functools
import math

import jax
import jax.numpy as jnp
from jax import lax
from jax.experimental import pallas as pl
from jax.experimental.pallas import tpu as pltpu
from jax.sharding import PartitionSpec as P

HD = 128
UNIT = 128
CAP = 512
N_Z = 8
N_TENSOR = 8
N_BLK = 32
ROWS = 2 * CAP
TILE = 256
HALF = CAP // 2
NEG = -(2.0**100)
LOWEST = -(2.0**99)
EXP_SCALE = math.log2(math.e) / math.sqrt(HD)
MESH = pl.DeviceIdType.MESH
NT = (((1,), (1,)), ((), ()))


def block_of(z, h, c):
    return lax.rem(z, N_Z) * 4 + h * 2 + c


def kernel(
    q_ref, k_ref, v_ref, w_ref, len_ref, ord_ref, out_ref,
    kv, q2, acc, top, bias, ob, og, wb, total, transit,
    loc, par_s, par_r, ring_s, ring_r, sib_s, sib_r, w_s, w_r, o_s, o_r, t_r, hs_s, h_r,
):
    b = lax.axis_index("blk")
    t = lax.axis_index("tensor")
    z = b // 4
    h = lax.rem(b // 2, 2)
    c = lax.rem(b, 2)
    y = t // 2
    x_lo = lax.rem(t, 2)
    other_b = block_of(z, 1 - h, c)
    sibling = {"blk": block_of(z, h, 1 - c), "tensor": t}
    partner = {"blk": other_b, "tensor": t}
    z_up = {"blk": block_of(z + 1, h, c), "tensor": t}
    z_down = {"blk": block_of(z + N_Z - 1, h, c), "tensor": t}
    my_cols = pl.ds(pl.multiple_of(h * HD, HD), HD)
    other_cols = pl.ds(pl.multiple_of((1 - h) * HD, HD), HD)
    my_head = 2 * t + h

    def tensor_at(step):
        return lax.rem(t + step, N_TENSOR)

    def remote(src, dst, send, recv, device):
        return pltpu.make_async_remote_copy(
            src_ref=src, dst_ref=dst, send_sem=send, recv_sem=recv,
            device_id=device, device_id_type=MESH,
        )

    own = [
        pltpu.make_async_copy(k_ref.at[:, my_cols], kv.at[b, 0], loc.at[0]),
        pltpu.make_async_copy(v_ref.at[:, my_cols], kv.at[b, 1], loc.at[1]),
        pltpu.make_async_copy(q_ref.at[:, my_cols], q2.at[pl.ds(0, CAP), pl.ds(0, HD)], loc.at[2]),
        pltpu.make_async_copy(
            w_ref.at[
                pl.ds(pl.multiple_of(c * HD, HD), HD), pl.ds(pl.multiple_of(t * CAP, CAP), CAP)
            ],
            wb.at[2 * t + c],
            loc.at[3],
        ),
    ]
    for copy in own:
        copy.start()

    barrier = pltpu.get_barrier_semaphore()
    peers = [z_up, z_down, sibling]
    peers += [{"blk": b, "tensor": tensor_at(d)} for d in range(1, N_TENSOR)]
    peers += [{"blk": other_b, "tensor": 2 * y + side} for side in range(2)]
    for peer in peers:
        pl.semaphore_signal(barrier, inc=1, device_id=peer, device_id_type=MESH)

    lane = lax.broadcasted_iota(jnp.int32, (UNIT, 128), 1)
    row = lax.broadcasted_iota(jnp.int32, (UNIT, 128), 0)
    lengths = jnp.broadcast_to(len_ref[...].astype(jnp.float32), (UNIT, N_BLK))
    orders = jnp.broadcast_to(ord_ref[...].astype(jnp.float32), (UNIT, N_BLK))
    holder = lane[:, :N_BLK] == row[:, :N_BLK] // 4
    unit_start = (lax.rem(row[:, :1], 4) * UNIT).astype(jnp.float32)
    my_len = jnp.sum(jnp.where(holder, lengths, 0.0), axis=1, keepdims=True)
    my_order = jnp.sum(jnp.where(holder, orders, 0.0), axis=1, keepdims=True)
    before = jnp.where(orders < my_order, lengths, 0.0)
    position = jnp.sum(before, axis=1, keepdims=True) + unit_start
    is_live = unit_start < my_len
    query_unit = jnp.where(lane < 4, b * 4 + lane, other_b * 4 + lane - 4)
    chosen = (query_unit == row) & (lane < 8)
    query_position = jnp.sum(jnp.where(chosen, position, 0.0), axis=0, keepdims=True)
    query_live = jnp.sum(jnp.where(chosen & is_live, 1.0, 0.0), axis=0, keepdims=True)
    bias[...] = jnp.where(is_live & (position < query_position), 0.0, NEG)
    tile_row = lax.broadcasted_iota(jnp.int32, (ROWS, HD), 0) // UNIT
    tile_lane = lax.broadcasted_iota(jnp.int32, (ROWS, HD), 1)
    q2[:, HD:] = jnp.where(tile_row == tile_lane, 1.0, 0.0).astype(jnp.bfloat16)

    pl.semaphore_wait(barrier, len(peers))
    for copy in own:
        copy.wait()

    def piece(slot, half):
        return kv.at[slot, :, pl.ds(pl.multiple_of(half * HALF, HALF), HALF), :]

    def ring_copy(slot, part, half, way, step):
        index = part * 16 + half * 8 + way * 4 + step
        device = z_up if way == 0 else z_down
        at = piece(slot, half)
        return remote(at, at, ring_s.at[index], ring_r.at[index], device)

    def sib_copy(slot, part, half, distance):
        index = part * 16 + half * 8 + distance
        at = piece(slot, half)
        return remote(at, at, sib_s.at[index], sib_r.at[index], sibling)

    def swap(half, which):
        rows = pl.ds(half * HALF, HALF)
        index = half * 2 + which
        source = v_ref if which else k_ref
        return remote(
            source.at[rows, other_cols],
            kv.at[b, which, rows, :],
            par_s.at[index],
            par_r.at[index],
            partner,
        )

    def swapped(half, which):
        at = kv.at[other_b, which, pl.ds(half * HALF, HALF), :]
        index = half * 2 + which
        remote(at, at, par_s.at[index], par_r.at[index], partner).wait_recv()

    swap_q = remote(
        q_ref.at[:, other_cols],
        q2.at[pl.ds(CAP, CAP), pl.ds(0, HD)],
        par_s.at[4],
        par_r.at[4],
        partner,
    )

    def send_own(half):
        for way in range(2):
            ring_copy(b, 0, half, way, 0).start()
        sib_copy(b, 0, half, 0).start()

    def send_swap(half):
        for which in range(2):
            swap(half, which).start()

    def send_swapped(half):
        for which in range(2):
            swapped(half, which)
        for way in range(2):
            ring_copy(other_b, 1, half, way, 0).start()
        sib_copy(other_b, 1, half, 0).start()

    def ring_step(part, hop, half, way, onward):
        side = lax.rem(h + part, 2)
        distance = N_Z - hop if way == 0 else hop
        slot = block_of(z + distance, side, c)
        ring_copy(slot, part, half, way, hop - 1).wait_recv()
        if onward is not None:

            @pl.when(onward)
            def _():
                ring_copy(slot, part, half, way, hop).start()

        sib_copy(slot, part, half, distance).start()

    def event(part, hop, half):
        ring_step(part, hop, half, 0, hop < 3)
        ring_step(part, hop, half, 1, hop < 3 + part)

    def send_fourth():
        for half in range(2):
            ring_copy(block_of(z + N_Z - 3, h, c), 0, half, 0, 3).start()

    def last_event(half):
        ring_step(0, 4, half, 0, None)
        ring_step(1, 4, half, 1, None)

    swap_q.start()
    send_own(0)
    top[...] = jnp.full_like(top, LOWEST)
    acc[...] = jnp.zeros_like(acc)

    square_row = lax.broadcasted_iota(jnp.int32, (UNIT, UNIT), 0)
    square_lane = lax.broadcasted_iota(jnp.int32, (UNIT, UNIT), 1)

    def diagonal(slot, first):
        def unit(i, carry):
            rows = pl.ds(pl.multiple_of((first + i) * UNIT, UNIT), UNIT)
            keys = pl.ds(pl.multiple_of(i * UNIT, UNIT), UNIT)
            k = kv[slot, 0, keys, :]
            v = kv[slot, 1, keys, :]
            s = lax.dot_general(q2[rows, :HD], k, NT, preferred_element_type=jnp.float32)
            s = jnp.where(square_lane <= square_row, s, NEG)
            old = top[rows, :]
            best = jnp.maximum(old, jnp.max(s, axis=1, keepdims=True))
            shrink = jnp.exp2((old - best) * EXP_SCALE)
            p = jnp.exp2((s - best) * EXP_SCALE).astype(jnp.bfloat16)
            top[rows, :] = best
            acc[rows, :] = acc[rows, :] * jnp.concatenate([shrink, shrink], axis=1) + jnp.dot(
                p,
                jnp.concatenate([v, jnp.ones_like(v)], axis=1),
                preferred_element_type=jnp.float32,
            )
            return carry

        lax.fori_loop(0, 4, unit, 0, unroll=True)

    diagonal(b, 0)
    send_swap(0)
    send_own(1)
    swap_q.wait_recv()
    send_swap(1)
    event(0, 1, 0)

    def w_copy(step):
        target = tensor_at(step)
        return remote(
            w_ref.at[
                pl.ds(pl.multiple_of(c * HD, HD), HD), pl.ds(pl.multiple_of(target * CAP, CAP), CAP)
            ],
            wb.at[2 * t + c],
            w_s.at[step - 1],
            w_r.at[step - 1],
            {"blk": b, "tensor": target},
        )

    def w_arrived(step):
        source = tensor_at(N_TENSOR - step)
        slot = wb.at[2 * source + c]
        remote(slot, slot, w_s.at[step - 1], w_r.at[step - 1], sibling).wait_recv()

    def w_sib(j):
        slot = wb.at[2 * j + c]
        return remote(slot, slot, w_s.at[7 + j], w_r.at[7 + j], sibling)

    def w_sib_arrived(j):
        slot = wb.at[2 * j + 1 - c]
        remote(slot, slot, w_s.at[7 + j], w_r.at[7 + j], sibling).wait_recv()

    def attend(slot_x, slot_y, half=None):
        start, count = (0, CAP) if half is None else (pl.multiple_of(half * HALF, HALF), HALF)
        rows = pl.ds(start, count)
        keys = jnp.concatenate([kv[slot_x, 0, rows, :], kv[slot_y, 0, rows, :]], axis=0)
        values = jnp.concatenate([kv[slot_x, 1, rows, :], kv[slot_y, 1, rows, :]], axis=0)
        fills = []
        for slot in (slot_x, slot_y):
            first = slot * 4 if half is None else slot * 4 + half * 2
            for j in range(count // UNIT):
                fills.append(jnp.broadcast_to(bias[pl.ds(first + j, 1), :], (UNIT, HD)))
        keys = jnp.concatenate([keys, jnp.concatenate(fills, axis=0).astype(jnp.bfloat16)], axis=1)
        values = jnp.concatenate([values, jnp.ones_like(values)], axis=1)
        for i in range(ROWS // TILE):
            rows = pl.ds(i * TILE, TILE)
            s = lax.dot_general(q2[rows, :], keys, NT, preferred_element_type=jnp.float32)
            old = top[rows, :]
            best = jnp.maximum(old, jnp.max(s, axis=1, keepdims=True))
            shrink = jnp.exp2((old - best) * EXP_SCALE)
            top[rows, :] = best
            p = jnp.concatenate(
                [
                    jnp.exp2((s[:, j * 128 : (j + 1) * 128] - best) * EXP_SCALE).astype(
                        jnp.bfloat16
                    )
                    for j in range(s.shape[1] // 128)
                ],
                axis=1,
            )
            update = jnp.dot(p, values, preferred_element_type=jnp.float32)
            acc[rows, :] = acc[rows, :] * jnp.concatenate([shrink, shrink], axis=1) + update

    def sib_wait(part, half, distance):
        side = lax.rem(h + part, 2)
        slot = block_of(z + distance, side, 1 - c)
        sib_copy(slot, part, half, distance).wait_recv()

    for half in range(2):
        sib_wait(0, half, 0)
    attend(b, block_of(z, h, 1 - c))

    def round_step(r, carry):
        part = 1 - lax.rem(r, 2)
        s = (r + 1) // 2 - part
        single = (4 - s) // 4

        def phase(ph, inner):
            core = lax.rem(c + ph, 2)

            @pl.when((ph == 0) & ((r == 1) | (r > 3)))
            def _():
                event(part, s, 1)

            @pl.when((ph == 0) & (r == 1))
            def _():
                send_swapped(0)

            @pl.when((ph == 1) & (r == 1))
            def _():
                send_swapped(1)
                event(0, 2, 0)

            @pl.when(r == 2)
            def _():
                event(0, 2, 1)
                for step in range(1, N_TENSOR):
                    w_copy(step).start()
                diagonal(other_b, 4)
                for half in range(2):
                    sib_wait(1, half, 0)

            @pl.when((ph == 0) & (r == 6))
            def _():
                send_fourth()

            @pl.when((ph == 1) & (r > 2) & (r < 6))
            def _():
                following = 1 - part
                event(following, (r + 2) // 2 - following, 0)

            @pl.when((ph == 1) & (r == 6))
            def _():
                event(1, 3, 0)
                for step in range(1, N_TENSOR):
                    w_arrived(step)
                for j in range(N_TENSOR):
                    w_sib(j).start()

            @pl.when(ph == 1)
            def _():
                for half in range(2):
                    sib_wait(part, half, N_Z - s)
                    sib_wait(part, half, s)

            side = lax.rem(h + part, 2)
            core_y = lax.rem(core + single, 2)
            attend(block_of(z + N_Z - s, side, core), block_of(z + s, side, core_y))
            return inner

        lax.fori_loop(0, 2 - single, phase, 0)
        return carry

    lax.fori_loop(1, 7, round_step, 0)

    def last_step(i, carry):
        far = i // 4
        half = lax.rem(i // 2, 2)
        core = lax.rem(c + i, 2)

        @pl.when(i == 2)
        def _():
            event(1, 3, 1)

        @pl.when(i == 4)
        def _():
            last_event(0)

        @pl.when(i == 6)
        def _():
            last_event(1)

        @pl.when(lax.rem(i, 2) == 1)
        def _():
            sib_wait(1 - far, half, 5 - far)
            sib_wait(1, half, 3 + far)

        side = lax.rem(h + 1 - far, 2)
        attend(block_of(z + 5 - far, side, core), block_of(z + 3 + far, 1 - h, core), half)
        return carry

    lax.fori_loop(0, 8, last_step, 0)

    def finish(half):
        for i in range(4):
            rows = pl.ds(half * CAP + i * UNIT, UNIT)
            unit_live = jnp.sum(
                jnp.where(lane[:1, :] == half * 4 + i, query_live, 0.0), axis=1, keepdims=True
            )
            o = jnp.where(unit_live > 0.0, acc[rows, :HD] / acc[rows, HD:], 0.0)
            ob[half, pl.ds(i * UNIT, UNIT), :] = o.astype(jnp.bfloat16)

    def plane(dy, e_hi, e_lo):
        side = lax.rem(h + e_hi, 2)
        column = lax.rem(x_lo + e_lo, 2)
        return {"blk": block_of(z, side, c), "tensor": 2 * lax.rem(y + dy, 4) + column}

    def head_at(dy, e_hi, e_lo):
        return (
            4 * lax.rem(y + dy, 4) + 2 * lax.rem(x_lo + e_lo, 2) + lax.rem(h + e_hi, 2)
        )

    def send_head(src, dy, e_hi, e_lo, head, index):
        return remote(src, og.at[head], o_s.at[index], o_r.at[head], plane(dy, e_hi, e_lo))

    def send_transit(dy, index):
        return remote(ob.at[1], transit.at[dy - 1], o_s.at[index], t_r.at[dy - 1], plane(dy, 0, 0))

    def arrived(head):
        remote(ob.at[0], og.at[head], o_s.at[0], o_r.at[head], partner).wait_recv()

    def transit_arrived(dy):
        slot = transit.at[dy - 1]
        remote(slot, slot, o_s.at[0], t_r.at[dy - 1], partner).wait_recv()

    def send_half(half, dy, head, index):
        at = og.at[head, pl.ds(half * HALF, HALF), :]
        return remote(at, at, hs_s.at[index], h_r.at[half * 16 + head], plane(dy, 0, 0))

    def half_arrived(half, head):
        at = og.at[head, pl.ds(half * HALF, HALF), :]
        remote(at, at, hs_s.at[0], h_r.at[half * 16 + head], partner).wait_recv()

    others = ((1, 0), (1, 1), (0, 1))
    steps = (1, 3, 2)

    finish(1)

    @pl.when(c == 0)
    def _():
        send_head(ob.at[1], 0, 1, 0, my_head, 0).start()
        send_head(ob.at[1], 0, 1, 1, my_head, 1).start()

    @pl.when(c == 1)
    def _():
        for i, dy in enumerate(steps):
            send_transit(dy, i).start()

    finish(0)

    @pl.when(c == 0)
    def _():
        send_head(ob.at[0], 0, 0, 1, my_head, 2).start()
        for i, dy in enumerate((1, 3)):
            send_head(ob.at[0], dy, 0, 0, my_head, 3 + i).start()

    @pl.when(c == 1)
    def _():
        for i, dy in enumerate(steps):
            send_head(ob.at[0], dy, 0, 0, my_head, 3 + i).start()
        for i, (e_hi, e_lo) in enumerate(others):
            send_head(ob.at[e_hi], 0, e_hi, e_lo, my_head, 6 + i).start()

    og[my_head] = ob[0]
    for j in range(N_TENSOR):
        w_sib_arrived(j)

    for half in range(2):
        for which in range(2):
            swap(half, which).wait_send()
    swap_q.wait_send()
    for step in range(1, N_TENSOR):
        w_copy(step).wait_send()
    for step in range(N_TENSOR):
        w_sib(step).wait_send()

    def sent(i, carry):
        part = i // 2
        half = lax.rem(i, 2)

        def sib_sent(distance, inner):
            sib_copy(0, part, half, distance).wait_send()
            return inner

        lax.fori_loop(0, N_Z, sib_sent, 0)
        for way in range(2):

            def ring_sent(step, inner, way=way):
                ring_copy(0, part, half, way, step).wait_send()
                return inner

            reach = 4 - part if way == 0 else 3 + part
            lax.fori_loop(0, reach, ring_sent, 0)
        return carry

    lax.fori_loop(0, 4, sent, 0)

    @pl.when(c == 0)
    def _():
        lanes = ((0, 0), (0, 1), (1, 1), (1, 0))
        for k, (e_hi, e_lo) in enumerate(lanes):
            if k > 0:
                head = head_at(0, e_hi, e_lo)
                arrived(head)
                for i, dy in enumerate((1, 3)):
                    send_head(og.at[head], dy, 0, 0, head, 3 + 2 * k + i).start()
        for k, (e_hi, e_lo) in enumerate(lanes):
            for i, dy in enumerate((1, 3)):
                head = head_at(4 - dy, e_hi, e_lo)
                arrived(head)
                send_half(i, dy, head, 2 * k + i).start()

    @pl.when(c == 1)
    def _():
        for k, dy in enumerate(steps):
            transit_arrived(dy)
            head = head_at(4 - dy, 0, 0)
            send_head(transit.at[dy - 1], 0, 1, 0, head, 9 + 3 * k).start()
            send_head(transit.at[dy - 1], 0, 1, 1, head, 10 + 3 * k).start()
            arrived(head)
            send_head(og.at[head], 0, 0, 1, head, 11 + 3 * k).start()

    for dy in (0, 1, 3, 2):
        for e_lo in range(2):
            first = 4 * lax.rem(y + dy, 4) + 2 * lax.rem(x_lo + e_lo, 2)

            for e_hi in range(2):
                head = head_at(dy, e_hi, e_lo)
                if dy == 2:
                    pl.when(c == 0)(functools.partial(half_arrived, 0, head))
                    pl.when(c == 0)(functools.partial(half_arrived, 1, head))
                if (e_hi, e_lo) != (0, 0):
                    pl.when(c == 1)(functools.partial(arrived, head))
            rows = jnp.concatenate([og[first], og[first + 1]], axis=1)
            weight = jnp.concatenate([wb[first], wb[first + 1]], axis=0)
            product = jnp.dot(rows, weight, preferred_element_type=jnp.float32)
            if (dy, e_lo) == (0, 0):
                total[...] = product
            elif (dy, e_lo) == (2, 1):
                out_ref[...] = (total[...] + product).astype(jnp.bfloat16)
            else:
                total[...] += product

    def head_sent(index, carry):
        send_head(ob.at[0], 1, 0, 0, my_head, index).wait_send()
        return carry

    def relay_sent(index, carry):
        send_half(0, 1, my_head, index).wait_send()
        return carry

    lax.fori_loop(0, 11 + 7 * c, head_sent, 0)
    lax.fori_loop(0, 8 * (1 - c), relay_sent, 0)


def body(queries, key_states, value_states, out_weight, lengths, cycle_order):
    any_space = pl.BlockSpec(memory_space=pl.ANY)
    vmem = pl.BlockSpec(memory_space=pltpu.VMEM)
    dma = pltpu.SemaphoreType.DMA
    return pl.pallas_call(
        kernel,
        out_shape=jax.ShapeDtypeStruct((CAP, CAP), jnp.bfloat16),
        in_specs=[any_space] * 4 + [vmem] * 2,
        out_specs=vmem,
        scratch_shapes=[
            pltpu.VMEM((N_BLK, 2, CAP, HD), jnp.bfloat16),
            pltpu.VMEM((ROWS, 2 * HD), jnp.bfloat16),
            pltpu.VMEM((ROWS, 2 * HD), jnp.float32),
            pltpu.VMEM((ROWS, HD), jnp.float32),
            pltpu.VMEM((UNIT, 128), jnp.float32),
            pltpu.VMEM((2, CAP, HD), jnp.bfloat16),
            pltpu.VMEM((2 * N_TENSOR, CAP, HD), jnp.bfloat16),
            pltpu.VMEM((2 * N_TENSOR, HD, CAP), jnp.bfloat16),
            pltpu.VMEM((CAP, CAP), jnp.float32),
            pltpu.VMEM((3, CAP, HD), jnp.bfloat16),
            dma((4,)),
            dma((5,)),
            dma((5,)),
            dma((32,)),
            dma((32,)),
            dma((32,)),
            dma((32,)),
            dma((15,)),
            dma((15,)),
            dma((18,)),
            dma((16,)),
            dma((3,)),
            dma((8,)),
            dma((32,)),
        ],
        compiler_params=pltpu.CompilerParams(
            collective_id=0, has_side_effects=True, vmem_limit_bytes=56 * 2**20
        ),
        name="ring_attention",
    )(queries, key_states, value_states, out_weight, lengths.reshape(1, N_BLK), cycle_order.reshape(1, N_BLK))


def solution(mesh):
    placed = (
        P("blk", "tensor"),
        P("blk", "tensor"),
        P("blk", "tensor"),
        P("tensor", None),
        P(),
        P(),
    )
    return jax.shard_map(
        body, mesh=mesh, in_specs=placed, out_specs=P("blk", "tensor"), check_vma=False
    )
```

```python
import functools
import math

import jax
import jax.numpy as jnp
from jax import lax
from jax.experimental import pallas as pl
from jax.experimental.pallas import tpu as pltpu
from jax.sharding import PartitionSpec as P

HD = 128
UNIT = 128
CAP = 512
N_Z = 8
N_TENSOR = 8
N_BLK = 32
ROWS = 2 * CAP
TILE = 256
HALF = CAP // 2
NEG = -(2.0**100)
LOWEST = -(2.0**99)
EXP_SCALE = math.log2(math.e) / math.sqrt(HD)
MESH = pl.DeviceIdType.MESH
NT = (((1,), (1,)), ((), ()))


def block_of(z, h, c):
    return lax.rem(z, N_Z) * 4 + h * 2 + c


def kernel(
    q_ref, k_ref, v_ref, w_ref, len_ref, ord_ref, out_ref,
    kv, q2, acc, top, bias, ob, og, wb, total, transit,
    loc, par_s, par_r, ring_s, ring_r, sib_s, sib_r, w_s, w_r, o_s, o_r, t_r, hs_s, h_r,
):
    b = lax.axis_index("blk")
    t = lax.axis_index("tensor")
    z = b // 4
    h = lax.rem(b // 2, 2)
    c = lax.rem(b, 2)
    y = t // 2
    x_lo = lax.rem(t, 2)
    other_b = block_of(z, 1 - h, c)
    sibling = {"blk": block_of(z, h, 1 - c), "tensor": t}
    partner = {"blk": other_b, "tensor": t}
    z_up = {"blk": block_of(z + 1, h, c), "tensor": t}
    z_down = {"blk": block_of(z + N_Z - 1, h, c), "tensor": t}
    my_cols = pl.ds(pl.multiple_of(h * HD, HD), HD)
    other_cols = pl.ds(pl.multiple_of((1 - h) * HD, HD), HD)
    my_head = 2 * t + h

    def tensor_at(step):
        return lax.rem(t + step, N_TENSOR)

    def remote(src, dst, send, recv, device):
        return pltpu.make_async_remote_copy(
            src_ref=src, dst_ref=dst, send_sem=send, recv_sem=recv,
            device_id=device, device_id_type=MESH,
        )

    own = [
        pltpu.make_async_copy(k_ref.at[:, my_cols], kv.at[b, 0], loc.at[0]),
        pltpu.make_async_copy(v_ref.at[:, my_cols], kv.at[b, 1], loc.at[1]),
        pltpu.make_async_copy(q_ref.at[:, my_cols], q2.at[pl.ds(0, CAP), pl.ds(0, HD)], loc.at[2]),
        pltpu.make_async_copy(
            w_ref.at[
                pl.ds(pl.multiple_of(c * HD, HD), HD), pl.ds(pl.multiple_of(t * CAP, CAP), CAP)
            ],
            wb.at[2 * t + c],
            loc.at[3],
        ),
    ]
    for copy in own:
        copy.start()

    barrier = pltpu.get_barrier_semaphore()
    peers = [z_up, z_down, sibling]
    peers += [{"blk": b, "tensor": tensor_at(d)} for d in range(1, N_TENSOR)]
    peers += [{"blk": other_b, "tensor": 2 * y + side} for side in range(2)]
    for peer in peers:
        pl.semaphore_signal(barrier, inc=1, device_id=peer, device_id_type=MESH)

    lane = lax.broadcasted_iota(jnp.int32, (UNIT, 128), 1)
    row = lax.broadcasted_iota(jnp.int32, (UNIT, 128), 0)
    lengths = jnp.broadcast_to(len_ref[...].astype(jnp.float32), (UNIT, N_BLK))
    orders = jnp.broadcast_to(ord_ref[...].astype(jnp.float32), (UNIT, N_BLK))
    holder = lane[:, :N_BLK] == row[:, :N_BLK] // 4
    unit_start = (lax.rem(row[:, :1], 4) * UNIT).astype(jnp.float32)
    my_len = jnp.sum(jnp.where(holder, lengths, 0.0), axis=1, keepdims=True)
    my_order = jnp.sum(jnp.where(holder, orders, 0.0), axis=1, keepdims=True)
    before = jnp.where(orders < my_order, lengths, 0.0)
    position = jnp.sum(before, axis=1, keepdims=True) + unit_start
    is_live = unit_start < my_len
    query_unit = jnp.where(lane < 4, b * 4 + lane, other_b * 4 + lane - 4)
    chosen = (query_unit == row) & (lane < 8)
    query_position = jnp.sum(jnp.where(chosen, position, 0.0), axis=0, keepdims=True)
    query_live = jnp.sum(jnp.where(chosen & is_live, 1.0, 0.0), axis=0, keepdims=True)
    bias[...] = jnp.where(is_live & (position < query_position), 0.0, NEG)
    tile_row = lax.broadcasted_iota(jnp.int32, (ROWS, HD), 0) // UNIT
    tile_lane = lax.broadcasted_iota(jnp.int32, (ROWS, HD), 1)
    q2[:, HD:] = jnp.where(tile_row == tile_lane, 1.0, 0.0).astype(jnp.bfloat16)

    pl.semaphore_wait(barrier, len(peers))
    for copy in own:
        copy.wait()

    def piece(slot, half):
        return kv.at[slot, :, pl.ds(pl.multiple_of(half * HALF, HALF), HALF), :]

    def ring_copy(slot, part, half, way, step):
        index = part * 16 + half * 8 + way * 4 + step
        device = z_up if way == 0 else z_down
        at = piece(slot, half)
        return remote(at, at, ring_s.at[index], ring_r.at[index], device)

    def sib_copy(slot, part, half, distance):
        index = part * 16 + half * 8 + distance
        at = piece(slot, half)
        return remote(at, at, sib_s.at[index], sib_r.at[index], sibling)

    def swap(half, which):
        rows = pl.ds(half * HALF, HALF)
        index = half * 2 + which
        source = v_ref if which else k_ref
        return remote(
            source.at[rows, other_cols],
            kv.at[b, which, rows, :],
            par_s.at[index],
            par_r.at[index],
            partner,
        )

    def swapped(half, which):
        at = kv.at[other_b, which, pl.ds(half * HALF, HALF), :]
        index = half * 2 + which
        remote(at, at, par_s.at[index], par_r.at[index], partner).wait_recv()

    swap_q = remote(
        q_ref.at[:, other_cols],
        q2.at[pl.ds(CAP, CAP), pl.ds(0, HD)],
        par_s.at[4],
        par_r.at[4],
        partner,
    )

    def send_own(half):
        for way in range(2):
            ring_copy(b, 0, half, way, 0).start()
        sib_copy(b, 0, half, 0).start()

    def send_swap(half):
        for which in range(2):
            swap(half, which).start()

    def send_swapped(half):
        for which in range(2):
            swapped(half, which)
        for way in range(2):
            ring_copy(other_b, 1, half, way, 0).start()
        sib_copy(other_b, 1, half, 0).start()

    def ring_step(part, hop, half, way, onward):
        side = lax.rem(h + part, 2)
        distance = N_Z - hop if way == 0 else hop
        slot = block_of(z + distance, side, c)
        ring_copy(slot, part, half, way, hop - 1).wait_recv()
        if onward is not None:

            @pl.when(onward)
            def _():
                ring_copy(slot, part, half, way, hop).start()

        sib_copy(slot, part, half, distance).start()

    def event(part, hop, half):
        ring_step(part, hop, half, 0, hop < 3)
        ring_step(part, hop, half, 1, hop < 3 + part)

    def send_fourth():
        for half in range(2):
            ring_copy(block_of(z + N_Z - 3, h, c), 0, half, 0, 3).start()

    def last_event(half):
        ring_step(0, 4, half, 0, None)
        ring_step(1, 4, half, 1, None)

    swap_q.start()
    send_own(0)
    top[...] = jnp.full_like(top, LOWEST)
    acc[...] = jnp.zeros_like(acc)

    square_row = lax.broadcasted_iota(jnp.int32, (UNIT, UNIT), 0)
    square_lane = lax.broadcasted_iota(jnp.int32, (UNIT, UNIT), 1)

    def diagonal(slot, first):
        def unit(i, carry):
            rows = pl.ds(pl.multiple_of((first + i) * UNIT, UNIT), UNIT)
            keys = pl.ds(pl.multiple_of(i * UNIT, UNIT), UNIT)
            k = kv[slot, 0, keys, :]
            v = kv[slot, 1, keys, :]
            s = lax.dot_general(q2[rows, :HD], k, NT, preferred_element_type=jnp.float32)
            s = jnp.where(square_lane <= square_row, s, NEG)
            old = top[rows, :]
            best = jnp.maximum(old, jnp.max(s, axis=1, keepdims=True))
            shrink = jnp.exp2((old - best) * EXP_SCALE)
            p = jnp.exp2((s - best) * EXP_SCALE).astype(jnp.bfloat16)
            top[rows, :] = best
            acc[rows, :] = acc[rows, :] * jnp.concatenate([shrink, shrink], axis=1) + jnp.dot(
                p,
                jnp.concatenate([v, jnp.ones_like(v)], axis=1),
                preferred_element_type=jnp.float32,
            )
            return carry

        lax.fori_loop(0, 4, unit, 0, unroll=True)

    diagonal(b, 0)
    send_swap(0)
    send_own(1)
    swap_q.wait_recv()
    send_swap(1)
    event(0, 1, 0)

    def w_copy(step):
        target = tensor_at(step)
        return remote(
            w_ref.at[
                pl.ds(pl.multiple_of(c * HD, HD), HD), pl.ds(pl.multiple_of(target * CAP, CAP), CAP)
            ],
            wb.at[2 * t + c],
            w_s.at[step - 1],
            w_r.at[step - 1],
            {"blk": b, "tensor": target},
        )

    def w_arrived(step):
        source = tensor_at(N_TENSOR - step)
        slot = wb.at[2 * source + c]
        remote(slot, slot, w_s.at[step - 1], w_r.at[step - 1], sibling).wait_recv()

    def w_sib(j):
        slot = wb.at[2 * j + c]
        return remote(slot, slot, w_s.at[7 + j], w_r.at[7 + j], sibling)

    def w_sib_arrived(j):
        slot = wb.at[2 * j + 1 - c]
        remote(slot, slot, w_s.at[7 + j], w_r.at[7 + j], sibling).wait_recv()

    def attend(slot_x, slot_y, half=None):
        start, count = (0, CAP) if half is None else (pl.multiple_of(half * HALF, HALF), HALF)
        rows = pl.ds(start, count)
        keys = jnp.concatenate([kv[slot_x, 0, rows, :], kv[slot_y, 0, rows, :]], axis=0)
        values = jnp.concatenate([kv[slot_x, 1, rows, :], kv[slot_y, 1, rows, :]], axis=0)
        fills = []
        for slot in (slot_x, slot_y):
            first = slot * 4 if half is None else slot * 4 + half * 2
            for j in range(count // UNIT):
                fills.append(jnp.broadcast_to(bias[pl.ds(first + j, 1), :], (UNIT, HD)))
        keys = jnp.concatenate([keys, jnp.concatenate(fills, axis=0).astype(jnp.bfloat16)], axis=1)
        values = jnp.concatenate([values, jnp.ones_like(values)], axis=1)
        for i in range(ROWS // TILE):
            rows = pl.ds(i * TILE, TILE)
            s = lax.dot_general(q2[rows, :], keys, NT, preferred_element_type=jnp.float32)
            old = top[rows, :]
            best = jnp.maximum(old, jnp.max(s, axis=1, keepdims=True))
            shrink = jnp.exp2((old - best) * EXP_SCALE)
            top[rows, :] = best
            p = jnp.concatenate(
                [
                    jnp.exp2((s[:, j * 128 : (j + 1) * 128] - best) * EXP_SCALE).astype(
                        jnp.bfloat16
                    )
                    for j in range(s.shape[1] // 128)
                ],
                axis=1,
            )
            update = jnp.dot(p, values, preferred_element_type=jnp.float32)
            acc[rows, :] = acc[rows, :] * jnp.concatenate([shrink, shrink], axis=1) + update

    def sib_wait(part, half, distance):
        side = lax.rem(h + part, 2)
        slot = block_of(z + distance, side, 1 - c)
        sib_copy(slot, part, half, distance).wait_recv()

    for half in range(2):
        sib_wait(0, half, 0)
    attend(b, block_of(z, h, 1 - c))

    def round_step(r, carry):
        part = 1 - lax.rem(r, 2)
        s = (r + 1) // 2 - part
        single = (4 - s) // 4

        def phase(ph, inner):
            core = lax.rem(c + ph, 2)

            @pl.when((ph == 0) & ((r == 1) | (r > 3)))
            def _():
                event(part, s, 1)

            @pl.when((ph == 0) & (r == 1))
            def _():
                send_swapped(0)

            @pl.when((ph == 1) & (r == 1))
            def _():
                send_swapped(1)
                event(0, 2, 0)

            @pl.when(r == 2)
            def _():
                event(0, 2, 1)
                for step in range(1, N_TENSOR):
                    w_copy(step).start()
                diagonal(other_b, 4)
                for half in range(2):
                    sib_wait(1, half, 0)

            @pl.when((ph == 0) & (r == 6))
            def _():
                send_fourth()

            @pl.when((ph == 1) & (r > 2) & (r < 6))
            def _():
                following = 1 - part
                event(following, (r + 2) // 2 - following, 0)

            @pl.when((ph == 1) & (r == 6))
            def _():
                event(1, 3, 0)
                for step in range(1, N_TENSOR):
                    w_arrived(step)
                for j in range(N_TENSOR):
                    w_sib(j).start()

            @pl.when(ph == 1)
            def _():
                for half in range(2):
                    sib_wait(part, half, N_Z - s)
                    sib_wait(part, half, s)

            side = lax.rem(h + part, 2)
            core_y = lax.rem(core + single, 2)
            attend(block_of(z + N_Z - s, side, core), block_of(z + s, side, core_y))
            return inner

        lax.fori_loop(0, 2 - single, phase, 0)
        return carry

    lax.fori_loop(1, 7, round_step, 0)

    def last_step(i, carry):
        far = i // 4
        half = lax.rem(i // 2, 2)
        core = lax.rem(c + i, 2)

        @pl.when(i == 2)
        def _():
            event(1, 3, 1)

        @pl.when(i == 4)
        def _():
            last_event(0)

        @pl.when(i == 6)
        def _():
            last_event(1)

        @pl.when(lax.rem(i, 2) == 1)
        def _():
            sib_wait(1 - far, half, 5 - far)
            sib_wait(1, half, 3 + far)

        side = lax.rem(h + 1 - far, 2)
        attend(block_of(z + 5 - far, side, core), block_of(z + 3 + far, 1 - h, core), half)
        return carry

    lax.fori_loop(0, 8, last_step, 0)

    def finish(half):
        for i in range(4):
            rows = pl.ds(half * CAP + i * UNIT, UNIT)
            unit_live = jnp.sum(
                jnp.where(lane[:1, :] == half * 4 + i, query_live, 0.0), axis=1, keepdims=True
            )
            o = jnp.where(unit_live > 0.0, acc[rows, :HD] / acc[rows, HD:], 0.0)
            ob[half, pl.ds(i * UNIT, UNIT), :] = o.astype(jnp.bfloat16)

    def plane(dy, e_hi, e_lo):
        side = lax.rem(h + e_hi, 2)
        column = lax.rem(x_lo + e_lo, 2)
        return {"blk": block_of(z, side, c), "tensor": 2 * lax.rem(y + dy, 4) + column}

    def head_at(dy, e_hi, e_lo):
        return (
            4 * lax.rem(y + dy, 4) + 2 * lax.rem(x_lo + e_lo, 2) + lax.rem(h + e_hi, 2)
        )

    def send_head(src, dy, e_hi, e_lo, head, index):
        return remote(src, og.at[head], o_s.at[index], o_r.at[head], plane(dy, e_hi, e_lo))

    def send_transit(dy, index):
        return remote(ob.at[1], transit.at[dy - 1], o_s.at[index], t_r.at[dy - 1], plane(dy, 0, 0))

    def arrived(head):
        remote(ob.at[0], og.at[head], o_s.at[0], o_r.at[head], partner).wait_recv()

    def transit_arrived(dy):
        slot = transit.at[dy - 1]
        remote(slot, slot, o_s.at[0], t_r.at[dy - 1], partner).wait_recv()

    def send_half(half, dy, head, index):
        at = og.at[head, pl.ds(half * HALF, HALF), :]
        return remote(at, at, hs_s.at[index], h_r.at[half * 16 + head], plane(dy, 0, 0))

    def half_arrived(half, head):
        at = og.at[head, pl.ds(half * HALF, HALF), :]
        remote(at, at, hs_s.at[0], h_r.at[half * 16 + head], partner).wait_recv()

    others = ((1, 0), (1, 1), (0, 1))
    near = (1, 3)

    finish(1)

    @pl.when(c == 0)
    def _():
        send_head(ob.at[1], 0, 1, 0, my_head, 0).start()
        send_head(ob.at[1], 0, 1, 1, my_head, 1).start()

    @pl.when(c == 1)
    def _():
        for i, dy in enumerate(near):
            send_transit(dy, i).start()
        send_transit(2, 16).start()

    finish(0)

    @pl.when(c == 0)
    def _():
        send_head(ob.at[0], 0, 0, 1, my_head, 2).start()
        for i, dy in enumerate((1, 3)):
            send_head(ob.at[0], dy, 0, 0, my_head, 3 + i).start()

    @pl.when(c == 1)
    def _():
        for i, dy in enumerate(near):
            send_head(ob.at[0], dy, 0, 0, my_head, 2 + i).start()
        for i, (e_hi, e_lo) in enumerate(others):
            send_head(ob.at[e_hi], 0, e_hi, e_lo, my_head, 4 + i).start()

    og[my_head] = ob[0]
    for j in range(N_TENSOR):
        w_sib_arrived(j)

    for half in range(2):
        for which in range(2):
            swap(half, which).wait_send()
    swap_q.wait_send()
    for step in range(1, N_TENSOR):
        w_copy(step).wait_send()
    for step in range(N_TENSOR):
        w_sib(step).wait_send()

    def sent(i, carry):
        part = i // 2
        half = lax.rem(i, 2)

        def sib_sent(distance, inner):
            sib_copy(0, part, half, distance).wait_send()
            return inner

        lax.fori_loop(0, N_Z, sib_sent, 0)
        for way in range(2):

            def ring_sent(step, inner, way=way):
                ring_copy(0, part, half, way, step).wait_send()
                return inner

            reach = 4 - part if way == 0 else 3 + part
            lax.fori_loop(0, reach, ring_sent, 0)
        return carry

    lax.fori_loop(0, 4, sent, 0)

    @pl.when(c == 0)
    def _():
        lanes = ((0, 0), (0, 1), (1, 1), (1, 0))
        for k, (e_hi, e_lo) in enumerate(lanes):
            if k > 0:
                head = head_at(0, e_hi, e_lo)
                arrived(head)
                for i, dy in enumerate((1, 3)):
                    send_head(og.at[head], dy, 0, 0, head, 3 + 2 * k + i).start()
        for k, (e_hi, e_lo) in enumerate(lanes):
            for i, dy in enumerate((1, 3)):
                head = head_at(4 - dy, e_hi, e_lo)
                arrived(head)
                send_half(i, dy, head, 2 * k + i).start()

    @pl.when(c == 1)
    def _():
        for k, dy in enumerate((1, 3, 2)):
            head = head_at(4 - dy, 0, 0)
            transit_arrived(dy)
            send_head(transit.at[dy - 1], 0, 1, 0, head, 7 + 3 * k).start()
            send_head(transit.at[dy - 1], 0, 1, 1, head, 8 + 3 * k).start()
            if dy == 2:
                half_arrived(0, head)
                half_arrived(1, head)
            else:
                arrived(head)
                send_half(k, dy, head, k).start()
            send_head(og.at[head], 0, 0, 1, head, 9 + 3 * k).start()

    for dy in (0, 1, 3, 2):
        for e_lo in range(2):
            first = 4 * lax.rem(y + dy, 4) + 2 * lax.rem(x_lo + e_lo, 2)

            for e_hi in range(2):
                head = head_at(dy, e_hi, e_lo)
                if dy == 2:
                    pl.when(c == 0)(functools.partial(half_arrived, 0, head))
                    pl.when(c == 0)(functools.partial(half_arrived, 1, head))
                if (e_hi, e_lo) != (0, 0):
                    pl.when(c == 1)(functools.partial(arrived, head))
            rows = jnp.concatenate([og[first], og[first + 1]], axis=1)
            weight = jnp.concatenate([wb[first], wb[first + 1]], axis=0)
            product = jnp.dot(rows, weight, preferred_element_type=jnp.float32)
            if (dy, e_lo) == (0, 0):
                total[...] = product
            elif (dy, e_lo) == (2, 1):
                out_ref[...] = (total[...] + product).astype(jnp.bfloat16)
            else:
                total[...] += product

    def head_sent(index, carry):
        send_head(ob.at[0], 1, 0, 0, my_head, index).wait_send()
        return carry

    def relay_sent(index, carry):
        send_half(0, 1, my_head, index).wait_send()
        return carry

    lax.fori_loop(0, 11 + 6 * c, head_sent, 0)
    lax.fori_loop(0, 8 - 6 * c, relay_sent, 0)


def body(queries, key_states, value_states, out_weight, lengths, cycle_order):
    any_space = pl.BlockSpec(memory_space=pl.ANY)
    vmem = pl.BlockSpec(memory_space=pltpu.VMEM)
    dma = pltpu.SemaphoreType.DMA
    return pl.pallas_call(
        kernel,
        out_shape=jax.ShapeDtypeStruct((CAP, CAP), jnp.bfloat16),
        in_specs=[any_space] * 4 + [vmem] * 2,
        out_specs=vmem,
        scratch_shapes=[
            pltpu.VMEM((N_BLK, 2, CAP, HD), jnp.bfloat16),
            pltpu.VMEM((ROWS, 2 * HD), jnp.bfloat16),
            pltpu.VMEM((ROWS, 2 * HD), jnp.float32),
            pltpu.VMEM((ROWS, HD), jnp.float32),
            pltpu.VMEM((UNIT, 128), jnp.float32),
            pltpu.VMEM((2, CAP, HD), jnp.bfloat16),
            pltpu.VMEM((2 * N_TENSOR, CAP, HD), jnp.bfloat16),
            pltpu.VMEM((2 * N_TENSOR, HD, CAP), jnp.bfloat16),
            pltpu.VMEM((CAP, CAP), jnp.float32),
            pltpu.VMEM((3, CAP, HD), jnp.bfloat16),
            dma((4,)),
            dma((5,)),
            dma((5,)),
            dma((32,)),
            dma((32,)),
            dma((32,)),
            dma((32,)),
            dma((15,)),
            dma((15,)),
            dma((17,)),
            dma((16,)),
            dma((3,)),
            dma((8,)),
            dma((32,)),
        ],
        compiler_params=pltpu.CompilerParams(
            collective_id=0, has_side_effects=True, vmem_limit_bytes=56 * 2**20
        ),
        name="ring_attention",
    )(queries, key_states, value_states, out_weight, lengths.reshape(1, N_BLK), cycle_order.reshape(1, N_BLK))


def solution(mesh):
    placed = (
        P("blk", "tensor"),
        P("blk", "tensor"),
        P("blk", "tensor"),
        P("tensor", None),
        P(),
        P(),
    )
    return jax.shard_map(
        body, mesh=mesh, in_specs=placed, out_specs=P("blk", "tensor"), check_vma=False
    )
```

```python
import functools
import math

import jax
import jax.numpy as jnp
from jax import lax
from jax.experimental import pallas as pl
from jax.experimental.pallas import tpu as pltpu
from jax.sharding import PartitionSpec as P

HD = 128
UNIT = 128
CAP = 512
N_Z = 8
N_TENSOR = 8
N_BLK = 32
ROWS = 2 * CAP
TILE = 256
HALF = CAP // 2
NEG = -(2.0**100)
LOWEST = -(2.0**99)
EXP_SCALE = math.log2(math.e) / math.sqrt(HD)
MESH = pl.DeviceIdType.MESH
NT = (((1,), (1,)), ((), ()))


def block_of(z, h, c):
    return lax.rem(z, N_Z) * 4 + h * 2 + c


def kernel(
    q_ref, k_ref, v_ref, w_ref, len_ref, ord_ref, out_ref,
    kv, q2, acc, top, bias, ob, og, wb, total, transit,
    loc, par_s, par_r, ring_s, ring_r, sib_s, sib_r, w_s, w_r, o_s, o_r, t_r, hs_s, h_r,
):
    b = lax.axis_index("blk")
    t = lax.axis_index("tensor")
    z = b // 4
    h = lax.rem(b // 2, 2)
    c = lax.rem(b, 2)
    y = t // 2
    x_lo = lax.rem(t, 2)
    other_b = block_of(z, 1 - h, c)
    sibling = {"blk": block_of(z, h, 1 - c), "tensor": t}
    partner = {"blk": other_b, "tensor": t}
    z_up = {"blk": block_of(z + 1, h, c), "tensor": t}
    z_down = {"blk": block_of(z + N_Z - 1, h, c), "tensor": t}
    my_cols = pl.ds(pl.multiple_of(h * HD, HD), HD)
    other_cols = pl.ds(pl.multiple_of((1 - h) * HD, HD), HD)
    my_head = 2 * t + h

    def tensor_at(step):
        return lax.rem(t + step, N_TENSOR)

    def remote(src, dst, send, recv, device):
        return pltpu.make_async_remote_copy(
            src_ref=src, dst_ref=dst, send_sem=send, recv_sem=recv,
            device_id=device, device_id_type=MESH,
        )

    own = [
        pltpu.make_async_copy(k_ref.at[:, my_cols], kv.at[b, 0], loc.at[0]),
        pltpu.make_async_copy(v_ref.at[:, my_cols], kv.at[b, 1], loc.at[1]),
        pltpu.make_async_copy(q_ref.at[:, my_cols], q2.at[pl.ds(0, CAP), pl.ds(0, HD)], loc.at[2]),
        pltpu.make_async_copy(
            w_ref.at[
                pl.ds(pl.multiple_of(c * HD, HD), HD), pl.ds(pl.multiple_of(t * CAP, CAP), CAP)
            ],
            wb.at[2 * t + c],
            loc.at[3],
        ),
    ]
    for copy in own:
        copy.start()

    barrier = pltpu.get_barrier_semaphore()
    peers = [z_up, z_down, sibling]
    peers += [{"blk": b, "tensor": tensor_at(d)} for d in range(1, N_TENSOR)]
    peers += [{"blk": other_b, "tensor": 2 * y + side} for side in range(2)]
    for peer in peers:
        pl.semaphore_signal(barrier, inc=1, device_id=peer, device_id_type=MESH)

    lane = lax.broadcasted_iota(jnp.int32, (UNIT, 128), 1)
    row = lax.broadcasted_iota(jnp.int32, (UNIT, 128), 0)
    lengths = jnp.broadcast_to(len_ref[...].astype(jnp.float32), (UNIT, N_BLK))
    orders = jnp.broadcast_to(ord_ref[...].astype(jnp.float32), (UNIT, N_BLK))
    holder = lane[:, :N_BLK] == row[:, :N_BLK] // 4
    unit_start = (lax.rem(row[:, :1], 4) * UNIT).astype(jnp.float32)
    my_len = jnp.sum(jnp.where(holder, lengths, 0.0), axis=1, keepdims=True)
    my_order = jnp.sum(jnp.where(holder, orders, 0.0), axis=1, keepdims=True)
    before = jnp.where(orders < my_order, lengths, 0.0)
    position = jnp.sum(before, axis=1, keepdims=True) + unit_start
    is_live = unit_start < my_len
    query_unit = jnp.where(lane < 4, b * 4 + lane, other_b * 4 + lane - 4)
    chosen = (query_unit == row) & (lane < 8)
    query_position = jnp.sum(jnp.where(chosen, position, 0.0), axis=0, keepdims=True)
    query_live = jnp.sum(jnp.where(chosen & is_live, 1.0, 0.0), axis=0, keepdims=True)
    bias[...] = jnp.where(is_live & (position < query_position), 0.0, NEG)
    tile_row = lax.broadcasted_iota(jnp.int32, (ROWS, HD), 0) // UNIT
    tile_lane = lax.broadcasted_iota(jnp.int32, (ROWS, HD), 1)
    q2[:, HD:] = jnp.where(tile_row == tile_lane, 1.0, 0.0).astype(jnp.bfloat16)

    pl.semaphore_wait(barrier, len(peers))
    for copy in own:
        copy.wait()

    def piece(slot, half):
        return kv.at[slot, :, pl.ds(pl.multiple_of(half * HALF, HALF), HALF), :]

    def ring_copy(slot, part, half, way, step):
        index = part * 16 + half * 8 + way * 4 + step
        device = z_up if way == 0 else z_down
        at = piece(slot, half)
        return remote(at, at, ring_s.at[index], ring_r.at[index], device)

    def sib_copy(slot, part, half, distance):
        index = part * 16 + half * 8 + distance
        at = piece(slot, half)
        return remote(at, at, sib_s.at[index], sib_r.at[index], sibling)

    def swap(half, which):
        rows = pl.ds(half * HALF, HALF)
        index = half * 2 + which
        source = v_ref if which else k_ref
        return remote(
            source.at[rows, other_cols],
            kv.at[b, which, rows, :],
            par_s.at[index],
            par_r.at[index],
            partner,
        )

    def swapped(half, which):
        at = kv.at[other_b, which, pl.ds(half * HALF, HALF), :]
        index = half * 2 + which
        remote(at, at, par_s.at[index], par_r.at[index], partner).wait_recv()

    swap_q = remote(
        q_ref.at[:, other_cols],
        q2.at[pl.ds(CAP, CAP), pl.ds(0, HD)],
        par_s.at[4],
        par_r.at[4],
        partner,
    )

    def send_own(half):
        for way in range(2):
            ring_copy(b, 0, half, way, 0).start()
        sib_copy(b, 0, half, 0).start()

    def send_swap(half):
        for which in range(2):
            swap(half, which).start()

    def send_swapped(half):
        for which in range(2):
            swapped(half, which)
        for way in range(2):
            ring_copy(other_b, 1, half, way, 0).start()
        sib_copy(other_b, 1, half, 0).start()

    def ring_step(part, hop, half, way, onward):
        side = lax.rem(h + part, 2)
        distance = N_Z - hop if way == 0 else hop
        slot = block_of(z + distance, side, c)
        ring_copy(slot, part, half, way, hop - 1).wait_recv()
        if onward is not None:

            @pl.when(onward)
            def _():
                ring_copy(slot, part, half, way, hop).start()

        sib_copy(slot, part, half, distance).start()

    def event(part, hop, half):
        ring_step(part, hop, half, 0, hop < 3)
        ring_step(part, hop, half, 1, hop < 3 + part)

    def send_fourth():
        for half in range(2):
            ring_copy(block_of(z + N_Z - 3, h, c), 0, half, 0, 3).start()

    def last_event(half):
        ring_step(0, 4, half, 0, None)
        ring_step(1, 4, half, 1, None)

    swap_q.start()
    send_own(0)
    top[...] = jnp.full_like(top, LOWEST)
    acc[...] = jnp.zeros_like(acc)

    square_row = lax.broadcasted_iota(jnp.int32, (UNIT, UNIT), 0)
    square_lane = lax.broadcasted_iota(jnp.int32, (UNIT, UNIT), 1)

    def diagonal(slot, first):
        def unit(i, carry):
            rows = pl.ds(pl.multiple_of((first + i) * UNIT, UNIT), UNIT)
            keys = pl.ds(pl.multiple_of(i * UNIT, UNIT), UNIT)
            k = kv[slot, 0, keys, :]
            v = kv[slot, 1, keys, :]
            s = lax.dot_general(q2[rows, :HD], k, NT, preferred_element_type=jnp.float32)
            s = jnp.where(square_lane <= square_row, s, NEG)
            old = top[rows, :]
            best = jnp.maximum(old, jnp.max(s, axis=1, keepdims=True))
            shrink = jnp.exp2((old - best) * EXP_SCALE)
            p = jnp.exp2((s - best) * EXP_SCALE).astype(jnp.bfloat16)
            top[rows, :] = best
            acc[rows, :] = acc[rows, :] * jnp.concatenate([shrink, shrink], axis=1) + jnp.dot(
                p,
                jnp.concatenate([v, jnp.ones_like(v)], axis=1),
                preferred_element_type=jnp.float32,
            )
            return carry

        lax.fori_loop(0, 4, unit, 0, unroll=True)

    diagonal(b, 0)
    send_swap(0)
    send_own(1)
    swap_q.wait_recv()
    send_swap(1)
    event(0, 1, 0)

    def w_copy(step):
        target = tensor_at(step)
        return remote(
            w_ref.at[
                pl.ds(pl.multiple_of(c * HD, HD), HD), pl.ds(pl.multiple_of(target * CAP, CAP), CAP)
            ],
            wb.at[2 * t + c],
            w_s.at[step - 1],
            w_r.at[step - 1],
            {"blk": b, "tensor": target},
        )

    def w_arrived(step):
        source = tensor_at(N_TENSOR - step)
        slot = wb.at[2 * source + c]
        remote(slot, slot, w_s.at[step - 1], w_r.at[step - 1], sibling).wait_recv()

    def w_sib(j):
        slot = wb.at[2 * j + c]
        return remote(slot, slot, w_s.at[7 + j], w_r.at[7 + j], sibling)

    def w_sib_arrived(j):
        slot = wb.at[2 * j + 1 - c]
        remote(slot, slot, w_s.at[7 + j], w_r.at[7 + j], sibling).wait_recv()

    def attend(slot_x, slot_y, half=None):
        start, count = (0, CAP) if half is None else (pl.multiple_of(half * HALF, HALF), HALF)
        rows = pl.ds(start, count)
        keys = jnp.concatenate([kv[slot_x, 0, rows, :], kv[slot_y, 0, rows, :]], axis=0)
        values = jnp.concatenate([kv[slot_x, 1, rows, :], kv[slot_y, 1, rows, :]], axis=0)
        fills = []
        for slot in (slot_x, slot_y):
            first = slot * 4 if half is None else slot * 4 + half * 2
            for j in range(count // UNIT):
                fills.append(jnp.broadcast_to(bias[pl.ds(first + j, 1), :], (UNIT, HD)))
        keys = jnp.concatenate([keys, jnp.concatenate(fills, axis=0).astype(jnp.bfloat16)], axis=1)
        values = jnp.concatenate([values, jnp.ones_like(values)], axis=1)
        for i in range(ROWS // TILE):
            rows = pl.ds(i * TILE, TILE)
            s = lax.dot_general(q2[rows, :], keys, NT, preferred_element_type=jnp.float32)
            old = top[rows, :]
            best = jnp.maximum(old, jnp.max(s, axis=1, keepdims=True))
            shrink = jnp.exp2((old - best) * EXP_SCALE)
            top[rows, :] = best
            p = jnp.concatenate(
                [
                    jnp.exp2((s[:, j * 128 : (j + 1) * 128] - best) * EXP_SCALE).astype(
                        jnp.bfloat16
                    )
                    for j in range(s.shape[1] // 128)
                ],
                axis=1,
            )
            update = jnp.dot(p, values, preferred_element_type=jnp.float32)
            acc[rows, :] = acc[rows, :] * jnp.concatenate([shrink, shrink], axis=1) + update

    def sib_wait(part, half, distance):
        side = lax.rem(h + part, 2)
        slot = block_of(z + distance, side, 1 - c)
        sib_copy(slot, part, half, distance).wait_recv()

    for half in range(2):
        sib_wait(0, half, 0)
    attend(b, block_of(z, h, 1 - c))

    def round_step(r, carry):
        part = 1 - lax.rem(r, 2)
        s = (r + 1) // 2 - part
        single = (4 - s) // 4

        def phase(ph, inner):
            core = lax.rem(c + ph, 2)

            @pl.when((ph == 0) & ((r == 1) | (r > 3)))
            def _():
                event(part, s, 1)

            @pl.when((ph == 0) & (r == 1))
            def _():
                send_swapped(0)

            @pl.when((ph == 1) & (r == 1))
            def _():
                send_swapped(1)
                event(0, 2, 0)

            @pl.when(r == 2)
            def _():
                event(0, 2, 1)
                for step in range(1, N_TENSOR):
                    w_copy(step).start()
                diagonal(other_b, 4)
                for half in range(2):
                    sib_wait(1, half, 0)

            @pl.when((ph == 0) & (r == 6))
            def _():
                send_fourth()

            @pl.when((ph == 1) & (r > 2) & (r < 6))
            def _():
                following = 1 - part
                event(following, (r + 2) // 2 - following, 0)

            @pl.when((ph == 1) & (r == 6))
            def _():
                event(1, 3, 0)
                for step in range(1, N_TENSOR):
                    w_arrived(step)
                for j in range(N_TENSOR):
                    w_sib(j).start()

            @pl.when(ph == 1)
            def _():
                for half in range(2):
                    sib_wait(part, half, N_Z - s)
                    sib_wait(part, half, s)

            side = lax.rem(h + part, 2)
            core_y = lax.rem(core + single, 2)
            attend(block_of(z + N_Z - s, side, core), block_of(z + s, side, core_y))
            return inner

        lax.fori_loop(0, 2 - single, phase, 0)
        return carry

    lax.fori_loop(1, 7, round_step, 0)

    def last_step(i, carry):
        far = i // 4
        half = lax.rem(i // 2, 2)
        core = lax.rem(c + i, 2)

        @pl.when(i == 2)
        def _():
            event(1, 3, 1)

        @pl.when(i == 4)
        def _():
            last_event(0)

        @pl.when(i == 6)
        def _():
            last_event(1)

        @pl.when(lax.rem(i, 2) == 1)
        def _():
            sib_wait(1 - far, half, 5 - far)
            sib_wait(1, half, 3 + far)

        side = lax.rem(h + 1 - far, 2)
        attend(block_of(z + 5 - far, side, core), block_of(z + 3 + far, 1 - h, core), half)
        return carry

    lax.fori_loop(0, 8, last_step, 0)

    def finish(half):
        for i in range(4):
            rows = pl.ds(half * CAP + i * UNIT, UNIT)
            unit_live = jnp.sum(
                jnp.where(lane[:1, :] == half * 4 + i, query_live, 0.0), axis=1, keepdims=True
            )
            o = jnp.where(unit_live > 0.0, acc[rows, :HD] / acc[rows, HD:], 0.0)
            ob[half, pl.ds(i * UNIT, UNIT), :] = o.astype(jnp.bfloat16)

    def plane(dy, e_hi, e_lo):
        side = lax.rem(h + e_hi, 2)
        column = lax.rem(x_lo + e_lo, 2)
        return {"blk": block_of(z, side, c), "tensor": 2 * lax.rem(y + dy, 4) + column}

    def head_at(dy, e_hi, e_lo):
        return (
            4 * lax.rem(y + dy, 4) + 2 * lax.rem(x_lo + e_lo, 2) + lax.rem(h + e_hi, 2)
        )

    def send_head(src, dy, e_hi, e_lo, head, index):
        return remote(src, og.at[head], o_s.at[index], o_r.at[head], plane(dy, e_hi, e_lo))

    def send_transit(dy, index):
        return remote(ob.at[1], transit.at[dy - 1], o_s.at[index], t_r.at[dy - 1], plane(dy, 0, 0))

    def arrived(head):
        remote(ob.at[0], og.at[head], o_s.at[0], o_r.at[head], partner).wait_recv()

    def transit_arrived(dy):
        slot = transit.at[dy - 1]
        remote(slot, slot, o_s.at[0], t_r.at[dy - 1], partner).wait_recv()

    def send_half(half, dy, head, index):
        at = og.at[head, pl.ds(half * HALF, HALF), :]
        return remote(at, at, hs_s.at[index], h_r.at[half * 16 + head], plane(dy, 0, 0))

    def half_arrived(half, head):
        at = og.at[head, pl.ds(half * HALF, HALF), :]
        remote(at, at, hs_s.at[0], h_r.at[half * 16 + head], partner).wait_recv()

    others = ((1, 0), (1, 1), (0, 1))
    near = (1, 3)

    finish(1)

    @pl.when(c == 0)
    def _():
        send_head(ob.at[1], 0, 1, 0, my_head, 0).start()
        send_head(ob.at[1], 0, 1, 1, my_head, 1).start()

    @pl.when(c == 1)
    def _():
        for i, dy in enumerate(near):
            send_transit(dy, i).start()
        for i, (e_hi, e_lo) in enumerate(others[:2]):
            send_head(ob.at[1], 0, e_hi, e_lo, my_head, 4 + i).start()
        send_transit(2, 16).start()

    finish(0)

    @pl.when(c == 0)
    def _():
        send_head(ob.at[0], 0, 0, 1, my_head, 2).start()
        for i, dy in enumerate((1, 3)):
            send_head(ob.at[0], dy, 0, 0, my_head, 3 + i).start()

    @pl.when(c == 1)
    def _():
        for i, dy in enumerate(near):
            send_head(ob.at[0], dy, 0, 0, my_head, 2 + i).start()
        send_head(ob.at[0], 0, 0, 1, my_head, 6).start()

    og[my_head] = ob[0]
    for j in range(N_TENSOR):
        w_sib_arrived(j)

    for half in range(2):
        for which in range(2):
            swap(half, which).wait_send()
    swap_q.wait_send()
    for step in range(1, N_TENSOR):
        w_copy(step).wait_send()
    for step in range(N_TENSOR):
        w_sib(step).wait_send()

    def sent(i, carry):
        part = i // 2
        half = lax.rem(i, 2)

        def sib_sent(distance, inner):
            sib_copy(0, part, half, distance).wait_send()
            return inner

        lax.fori_loop(0, N_Z, sib_sent, 0)
        for way in range(2):

            def ring_sent(step, inner, way=way):
                ring_copy(0, part, half, way, step).wait_send()
                return inner

            reach = 4 - part if way == 0 else 3 + part
            lax.fori_loop(0, reach, ring_sent, 0)
        return carry

    lax.fori_loop(0, 4, sent, 0)

    @pl.when(c == 0)
    def _():
        lanes = ((0, 0), (0, 1), (1, 1), (1, 0))
        for k, (e_hi, e_lo) in enumerate(lanes):
            if k > 0:
                head = head_at(0, e_hi, e_lo)
                arrived(head)
                for i, dy in enumerate((1, 3)):
                    send_head(og.at[head], dy, 0, 0, head, 3 + 2 * k + i).start()
        for k, (e_hi, e_lo) in enumerate(lanes):
            for i, dy in enumerate((1, 3)):
                head = head_at(4 - dy, e_hi, e_lo)
                arrived(head)
                send_half(i, dy, head, 2 * k + i).start()

    @pl.when(c == 1)
    def _():
        for k, dy in enumerate((1, 3, 2)):
            head = head_at(4 - dy, 0, 0)
            transit_arrived(dy)
            send_head(transit.at[dy - 1], 0, 1, 0, head, 7 + 3 * k).start()
            send_head(transit.at[dy - 1], 0, 1, 1, head, 8 + 3 * k).start()
            if dy == 2:
                half_arrived(0, head)
                half_arrived(1, head)
            else:
                arrived(head)
                send_half(k, dy, head, k).start()
            send_head(og.at[head], 0, 0, 1, head, 9 + 3 * k).start()

    for dy in (0, 1, 3, 2):
        for e_lo in range(2):
            first = 4 * lax.rem(y + dy, 4) + 2 * lax.rem(x_lo + e_lo, 2)

            for e_hi in range(2):
                head = head_at(dy, e_hi, e_lo)
                if dy == 2:
                    pl.when(c == 0)(functools.partial(half_arrived, 0, head))
                    pl.when(c == 0)(functools.partial(half_arrived, 1, head))
                if (e_hi, e_lo) != (0, 0):
                    pl.when(c == 1)(functools.partial(arrived, head))
            rows = jnp.concatenate([og[first], og[first + 1]], axis=1)
            weight = jnp.concatenate([wb[first], wb[first + 1]], axis=0)
            product = jnp.dot(rows, weight, preferred_element_type=jnp.float32)
            if (dy, e_lo) == (0, 0):
                total[...] = product
            elif (dy, e_lo) == (2, 1):
                out_ref[...] = (total[...] + product).astype(jnp.bfloat16)
            else:
                total[...] += product

    def head_sent(index, carry):
        send_head(ob.at[0], 1, 0, 0, my_head, index).wait_send()
        return carry

    def relay_sent(index, carry):
        send_half(0, 1, my_head, index).wait_send()
        return carry

    lax.fori_loop(0, 11 + 6 * c, head_sent, 0)
    lax.fori_loop(0, 8 - 6 * c, relay_sent, 0)


def body(queries, key_states, value_states, out_weight, lengths, cycle_order):
    any_space = pl.BlockSpec(memory_space=pl.ANY)
    vmem = pl.BlockSpec(memory_space=pltpu.VMEM)
    dma = pltpu.SemaphoreType.DMA
    return pl.pallas_call(
        kernel,
        out_shape=jax.ShapeDtypeStruct((CAP, CAP), jnp.bfloat16),
        in_specs=[any_space] * 4 + [vmem] * 2,
        out_specs=vmem,
        scratch_shapes=[
            pltpu.VMEM((N_BLK, 2, CAP, HD), jnp.bfloat16),
            pltpu.VMEM((ROWS, 2 * HD), jnp.bfloat16),
            pltpu.VMEM((ROWS, 2 * HD), jnp.float32),
            pltpu.VMEM((ROWS, HD), jnp.float32),
            pltpu.VMEM((UNIT, 128), jnp.float32),
            pltpu.VMEM((2, CAP, HD), jnp.bfloat16),
            pltpu.VMEM((2 * N_TENSOR, CAP, HD), jnp.bfloat16),
            pltpu.VMEM((2 * N_TENSOR, HD, CAP), jnp.bfloat16),
            pltpu.VMEM((CAP, CAP), jnp.float32),
            pltpu.VMEM((3, CAP, HD), jnp.bfloat16),
            dma((4,)),
            dma((5,)),
            dma((5,)),
            dma((32,)),
            dma((32,)),
            dma((32,)),
            dma((32,)),
            dma((15,)),
            dma((15,)),
            dma((17,)),
            dma((16,)),
            dma((3,)),
            dma((8,)),
            dma((32,)),
        ],
        compiler_params=pltpu.CompilerParams(
            collective_id=0, has_side_effects=True, vmem_limit_bytes=56 * 2**20
        ),
        name="ring_attention",
    )(queries, key_states, value_states, out_weight, lengths.reshape(1, N_BLK), cycle_order.reshape(1, N_BLK))


def solution(mesh):
    placed = (
        P("blk", "tensor"),
        P("blk", "tensor"),
        P("blk", "tensor"),
        P("tensor", None),
        P(),
        P(),
    )
    return jax.shard_map(
        body, mesh=mesh, in_specs=placed, out_specs=P("blk", "tensor"), check_vma=False
    )
```
